256 devices in a mesh: aux: 16 (over x, z_hi, core), orb: 16 (over z_lo, y).
Axes of the slice: x: 4, y: 4, z: 8 (z_hi: 2, z_lo: 4; z = z_hi * 4 + z_lo), core: 2. Of those that a mesh axis runs over, the one named last changes fastest.
Arguments:
- fitted: bfloat16 [512, 768, 2048], P('aux', 'orb'), may hold values from -0.23925781 to 0.23925781
- screen: int32 [128, 16], P('aux'), may hold values 0 or 1
- block_sizes: int32 [128], P('aux'), may hold values from 1 to 4, as said below
Outputs:
- exchange_matrix: float32 [2048, 2048], P(('aux', 'orb'))
The draws below stay inside these ranges and needn't reach their ends.
Inputs may be any that keep to these rules, and one draw needn't show every extreme that they name: The first block_sizes[b] of the 4 auxiliary functions of block b are live; the others are ignored.
All inputs are finite; a program needn't handle non-finite values. No bound on the sum of `screen` on one device may be relied on, other than what follows from the above.
Results may differ from the reference program's by a relative error of at most 0.0003.
Values may be sent and summed in bfloat16 or wider, within the bound.
No kernel may reach another device: no remote copies, remote signals or barrier semaphores. Data moves between devices by JAX's collectives and lax.ppermute only.
A program may use at most 128 MiB of HBM per device.

```python
import jax
import jax.numpy as jnp
from jax import lax

NBF = 2048
NOCC = 768
AUX_PER_BLOCK = 4
BASIS_PER_TILE = 128
NAUX = 512
NQBLK = 128
BLK_DEV = 8
NTILE = 16


def draw_block_sizes(key, part):
    key = jax.random.fold_in(key, 11)
    key_caps, key_raw, key_full = jax.random.split(key, 3)
    device_caps = jax.random.randint(key_caps, (NQBLK // BLK_DEV,), 1, AUX_PER_BLOCK + 1)
    block_caps = jnp.repeat(device_caps, BLK_DEV)
    raw_values = jax.random.randint(key_raw, (NQBLK,), 0, AUX_PER_BLOCK * AUX_PER_BLOCK * 64)
    drawn = 1 + raw_values % block_caps
    full_block = jax.random.randint(key_full, (), 0, NQBLK)
    drawn = jnp.where(jnp.arange(NQBLK) == full_block, AUX_PER_BLOCK, drawn)
    return drawn.astype(jnp.int32)


def plant(result, own_key, smallest, top_value):
    index_at = [jax.random.randint(jax.random.fold_in(own_key, axis), (), 0, length) for axis, length in enumerate(result.shape)]
    main_axis = result.shape.index(max(result.shape))
    beside = index_at[:main_axis] + [(index_at[main_axis] + 1) % result.shape[main_axis]] + index_at[main_axis + 1:]
    return result.at[tuple(index_at)].set(smallest).at[tuple(beside)].set(top_value)


def block_scale(stream_key, dims, cuts, least, top_value):
    def one(dim, shards_of):
        steps = jax.random.uniform(jax.random.fold_in(jax.random.fold_in(stream_key, 6), dim), (shards_of,), jnp.float32, least / len(cuts), top_value / len(cuts))
        return jnp.repeat(jnp.exp(steps), dims[dim] // shards_of).reshape((-1,) + (1,) * (len(dims) - dim - 1))

    loudness = one(*cuts[0])
    for cut in cuts[1:]:
        loudness = loudness * one(*cut)
    return loudness


def bell_draw(key, extent, deviation, most, pieces=(), held_as=jnp.bfloat16):
    values = jax.random.normal(key, extent, jnp.float32) * deviation
    if len(pieces) > 0:
        values = block_scale(key, extent, pieces, -0.22, 0.18) * values
    return jnp.clip(values, min=-most, max=most).astype(held_as)


def setup_inputs(seed: int = 0) -> dict:
    arg_keys = jax.random.split(jax.random.key(seed), 4)
    fitted = bell_draw(arg_keys[0], (NAUX, NOCC, NBF), (1.0 / (NAUX * NOCC) ** 0.25), 0.23925781, ((0, 16), (1, 16)))
    screen = plant((jax.random.randint(arg_keys[1], (NQBLK, NTILE), 0, 4) < 3).astype(jnp.int32), jax.random.fold_in(arg_keys[1], 1), 0, 1)
    block_sizes = draw_block_sizes(jax.random.fold_in(arg_keys[3], 71), 0)
    return {"fitted": fitted, "screen": screen, "block_sizes": block_sizes}


def reference(fitted, screen, block_sizes):
    active_rows = (jnp.arange(NAUX, dtype=jnp.int32) % AUX_PER_BLOCK) < jnp.repeat(block_sizes, AUX_PER_BLOCK)
    retain_mask = jnp.repeat(jnp.repeat(screen, BASIS_PER_TILE, axis=1), AUX_PER_BLOCK, axis=0) * active_rows[:, None].astype(jnp.int32)

    def add_block(running, block_index):
        block_rows = lax.dynamic_slice_in_dim(fitted, (block_index * AUX_PER_BLOCK).astype(jnp.int32), AUX_PER_BLOCK, 0).astype(jnp.float32)
        block_keep = lax.dynamic_slice_in_dim(retain_mask, (block_index * AUX_PER_BLOCK).astype(jnp.int32), AUX_PER_BLOCK, 0).astype(jnp.float32)
        weighted = (block_rows * block_keep[:, None, :]).reshape(AUX_PER_BLOCK * NOCC, NBF)
        return running + jnp.dot(weighted.T, weighted, preferred_element_type=jnp.float32), None

    running, unused = lax.scan(add_block, jnp.zeros((NBF, NBF), jnp.float32), jnp.arange(NQBLK, dtype=jnp.int32))
    return running
```

```python
import functools

import jax
import jax.numpy as jnp
import numpy as np
from jax import lax
from jax.experimental import pallas as pl
from jax.experimental.pallas import tpu as pltpu
from jax.sharding import Mesh, PartitionSpec as P

AUX_PER_BLOCK = 4
BASIS_PER_TILE = 128
SIZES = (4, 2, 2, 4, 4)
AXES = ("x", "zh", "core", "zl", "y")
FULL = 32767.0
HALF = 1024
PIECE = 64
SCALE_ROWS = 16
VMEM_LIMIT = 56 << 20


def partner_a(v, core):
    return v ^ 1 if core == 0 else 3 - v


def partner_b(v, core):
    return 3 - v if core == 0 else v ^ 1


PARTNERS = {
    "core": lambda x, y, core: (x, y, 1 - core),
    "x1": lambda x, y, core: (partner_a(x, core), y, core),
    "x2": lambda x, y, core: (partner_b(x, core), y, core),
    "y1": lambda x, y, core: (x, partner_a(y, core), core),
    "y2": lambda x, y, core: (x, partner_b(y, core), core),
}


def swap(value, step):
    pairs = []
    for here in range(256):
        x, zh, core, zl, y = (int(v) for v in np.unravel_index(here, SIZES))
        to_x, to_y, to_core = PARTNERS[step](x, y, core)
        pairs.append((here, int(np.ravel_multi_index((to_x, zh, to_core, zl, to_y), SIZES))))
    return lax.ppermute(value, AXES, pairs)


def exponent_of(largest):
    return jnp.clip(jnp.floor(jnp.log2(largest)) + 1.0, -100.0, 100.0)


def to_codes(values, exponent):
    return jnp.round(values * (jnp.exp2(-exponent) * FULL)).astype(jnp.int32).astype(jnp.int16)


def write_pieces(load, count, payload_ref):
    row = lax.broadcasted_iota(jnp.int32, (SCALE_ROWS, HALF), 0)
    scales = jnp.zeros((SCALE_ROWS, HALF), jnp.float32)
    for k in range(count):
        values = load(k)
        exponent = exponent_of(jnp.max(jnp.abs(values), axis=0, keepdims=True))
        payload_ref[k * PIECE : (k + 1) * PIECE, :] = to_codes(values, exponent)
        scales = jnp.where(row == k, exponent, scales)
    payload_ref[count * PIECE :, :] = scales.astype(jnp.int32).astype(jnp.int16)


def read_scales(payload_ref, count):
    exponents = payload_ref[count * PIECE :, :].astype(jnp.int32).astype(jnp.float32)
    return jnp.exp2(exponents) * (1.0 / FULL)


def read_piece(payload_ref, scales, k):
    codes = payload_ref[k * PIECE : (k + 1) * PIECE, :].astype(jnp.int32).astype(jnp.float32)
    return codes * scales[k : k + 1, :]


def mask_rows(fitted_ref, keep_ref, masked_ref):
    for q in range(fitted_ref.shape[0]):
        masked_ref[q * 48 : (q + 1) * 48, :] = fitted_ref[q] * keep_ref[q : q + 1, :]


def product(masked_ref, core, x, column, width):
    tiles = [
        masked_ref[:, pl.ds(pl.multiple_of(((x * 2 + zh) * 2 + core) * 128, 128), 128)]
        for zh in range(2)
    ]
    return lax.dot_general(
        jnp.concatenate(tiles, axis=1),
        masked_ref[:, column : column + width],
        (((0,), (0,)), ((), ())),
        preferred_element_type=jnp.float32,
    )


def place(result, x, out_ref, column, width, add_ref=None):
    for zh in range(2):
        for zl in range(4):
            for y in range(4):
                source = zh * 128 + zl * 32 + y * 8
                target = (zh * 4 + zl) * 8
                values = result[source : source + 8, :]
                if add_ref is not None:
                    values = values + add_ref[x * 4 + y, target : target + 8, column : column + width]
                out_ref[x * 4 + y, target : target + 8, column : column + width] = values


def own_kernel(index_ref, fitted_ref, keep_ref, first_ref, second_ref, masked_ref):
    mask_rows(fitted_ref, keep_ref, masked_ref)
    for stream, out_ref in enumerate((first_ref, second_ref)):
        for x in range(4):
            result = product(masked_ref, index_ref[0], x, stream * HALF, HALF)
            place(result, x, out_ref, 0, HALF)


def other_kernel(stream, index_ref, fitted_ref, keep_ref, own_ref, state_ref, payload_ref, masked_ref, total_ref):
    mask_rows(fitted_ref, keep_ref, masked_ref)
    for x in range(4):
        result = product(masked_ref, index_ref[0], x, stream * HALF, HALF)
        place(result, x, total_ref, 0, HALF, own_ref)
    slots = []
    for major in range(4):
        for minor in range(4):
            i, j = (major, minor) if stream == 0 else (minor, major)
            slots.append(index_ref[1 + i] * 4 + index_ref[5 + j])
    for k in range(8):
        state_ref[k] = total_ref[slots[k]]
    write_pieces(lambda k: total_ref[slots[8 + k]], 8, payload_ref)


def step_kernel(count, state_ref, got_ref, next_ref, payload_ref):
    scales = read_scales(got_ref, count)
    half = count // 2
    for k in range(half):
        next_ref[k] = state_ref[k] + read_piece(got_ref, scales, k)
    write_pieces(lambda k: state_ref[half + k] + read_piece(got_ref, scales, half + k), half, payload_ref)


def pack_kernel(state_x, got_x, state_y, got_y, out_ref):
    sums = [
        state_ref[0] + read_piece(got_ref, read_scales(got_ref, 1), 0)
        for state_ref, got_ref in ((state_x, got_x), (state_y, got_y))
    ]
    lane = lax.broadcasted_iota(jnp.int32, (16, 128), 1)
    for z in range(8):
        rows = jnp.concatenate([s[z * 8 : (z + 1) * 8, :] for s in sums], axis=0)
        exponents = jnp.zeros((16, 128), jnp.float32)
        for g in range(8):
            values = rows[:, g * 128 : (g + 1) * 128]
            exponent = exponent_of(jnp.max(jnp.abs(values), axis=1, keepdims=True))
            out_ref[z, :, g * 128 : (g + 1) * 128] = to_codes(values, exponent)
            exponents = jnp.where(lane == g, exponent, exponents)
        out_ref[z, :, HALF:] = exponents.astype(jnp.int32).astype(jnp.int16)


def unpack_kernel(got_ref, out_ref):
    total = [jnp.zeros((16, 128), jnp.float32) for _ in range(8)]
    for z in range(8):
        scales = jnp.exp2(got_ref[z, :, HALF:].astype(jnp.int32).astype(jnp.float32)) * (1.0 / FULL)
        for g in range(8):
            codes = got_ref[z, :, g * 128 : (g + 1) * 128].astype(jnp.int32).astype(jnp.float32)
            total[g] = total[g] + codes * scales[:, g : g + 1]
    for g in range(8):
        out_ref[:, g * 128 : (g + 1) * 128] = total[g][:8]
        out_ref[:, HALF + g * 128 : HALF + (g + 1) * 128] = total[g][8:]


SMEM = pl.BlockSpec(memory_space=pltpu.SMEM)
VMEM = pl.BlockSpec(memory_space=pltpu.VMEM)


def call(kernel, inputs, outputs, scratch=(), flops=0):
    specs = [SMEM if a.dtype == jnp.int32 else VMEM for a in inputs]
    moved = sum(int(np.prod(a.shape)) * a.dtype.itemsize for a in (*inputs, *outputs))
    return pl.pallas_call(
        kernel,
        in_specs=specs,
        out_specs=[VMEM] * len(outputs),
        out_shape=list(outputs),
        scratch_shapes=list(scratch),
        compiler_params=pltpu.CompilerParams(vmem_limit_bytes=VMEM_LIMIT),
        cost_estimate=pl.CostEstimate(flops=flops, bytes_accessed=moved, transcendentals=0),
    )(*inputs)


def state_shape(count):
    return jax.ShapeDtypeStruct((count, PIECE, HALF), jnp.float32)


def payload_shape(count):
    return jax.ShapeDtypeStruct((count * PIECE + SCALE_ROWS, HALF), jnp.int16)


def on_device(fitted, screen, block_sizes):
    rows = fitted.shape[0]
    live = jnp.arange(rows, dtype=jnp.int32) % AUX_PER_BLOCK < jnp.repeat(block_sizes, AUX_PER_BLOCK)
    kept = jnp.repeat(screen, AUX_PER_BLOCK, axis=0) * live[:, None].astype(jnp.int32)

    def spread(tiles):
        return jnp.repeat(tiles.astype(jnp.bfloat16), BASIS_PER_TILE, axis=1)

    other_fitted = swap(fitted, "core")
    other_kept = swap(kept, "core")

    x, core, y = lax.axis_index("x"), lax.axis_index("core"), lax.axis_index("y")

    def order(v):
        first = jnp.where(core == 0, v ^ 1, 3 - v)
        second = lambda u: jnp.where(core == 0, 3 - u, u ^ 1)
        return [v, second(v), first, second(first)]

    index = jnp.stack([core, *order(x), *order(y)]).astype(jnp.int32)
    masked = pltpu.VMEM((rows * 48, 2 * HALF), jnp.bfloat16)
    whole = pltpu.VMEM((16, PIECE, HALF), jnp.float32)
    work = 2 * rows * 48 * HALF * HALF
    own = call(own_kernel, (index, fitted, spread(kept)), (state_shape(16),) * 2, (masked,), 2 * work)
    streams = []
    for stream in range(2):
        streams.append(
            call(
                functools.partial(other_kernel, stream),
                (index, other_fitted, spread(other_kept), own[stream]),
                (state_shape(8), payload_shape(8)),
                (masked, whole),
                work,
            )
        )
    got = [swap(payload, step) for (_, payload), step in zip(streams, ("x1", "y1"))]
    for steps, count in ((("x2", "y2"), 8), (("y1", "x1"), 4), (("y2", "x2"), 2)):
        streams = [
            call(
                functools.partial(step_kernel, count),
                (state, payload),
                (state_shape(count // 2), payload_shape(count // 2)),
            )
            for (state, _), payload in zip(streams, got)
        ]
        got = [swap(payload, step) for (_, payload), step in zip(streams, steps)]
    message = call(
        pack_kernel,
        (streams[0][0], got[0], streams[1][0], got[1]),
        (jax.ShapeDtypeStruct((8, 16, HALF + 128), jnp.int16),),
    )[0]
    message = lax.all_to_all(message, ("zh", "zl"), 0, 0, tiled=True)
    return call(unpack_kernel, (message,), (jax.ShapeDtypeStruct((8, 2 * HALF), jnp.float32),))[0]


def solution(mesh):
    physical = Mesh(mesh.devices.reshape(SIZES), AXES)
    return jax.shard_map(
        on_device,
        mesh=physical,
        in_specs=(P(("x", "zh", "core"), ("zl", "y"), None), P(("x", "zh", "core"), None), P(("x", "zh", "core"))),
        out_specs=P(AXES, None),
        check_vma=False,
    )
```

```python
import functools

import jax
import jax.numpy as jnp
import numpy as np
from jax import lax
from jax.experimental import pallas as pl
from jax.experimental.pallas import tpu as pltpu
from jax.sharding import Mesh, PartitionSpec as P

AUX_PER_BLOCK = 4
BASIS_PER_TILE = 128
TILES = 16
SIZES = (4, 2, 2, 4, 4)
AXES = ("x", "zh", "core", "zl", "y")
FULL = 32767.0
HALF = 1024
PIECE = 64
OWN_LIMIT = 42
OTHER_LIMIT = 22
SCALE_ROWS = 16


def partner_a(v, core):
    return v ^ 1 if core == 0 else 3 - v


def partner_b(v, core):
    return 3 - v if core == 0 else v ^ 1


PARTNERS = {
    "core": lambda x, y, core: (x, y, 1 - core),
    "x1": lambda x, y, core: (partner_a(x, core), y, core),
    "x2": lambda x, y, core: (partner_b(x, core), y, core),
    "y1": lambda x, y, core: (x, partner_a(y, core), core),
    "y2": lambda x, y, core: (x, partner_b(y, core), core),
}


def swap(value, step):
    pairs = []
    for here in range(256):
        x, zh, core, zl, y = (int(v) for v in np.unravel_index(here, SIZES))
        to_x, to_y, to_core = PARTNERS[step](x, y, core)
        pairs.append((here, int(np.ravel_multi_index((to_x, zh, to_core, zl, to_y), SIZES))))
    return lax.ppermute(value, AXES, pairs)


def exponent_of(largest):
    return jnp.clip(jnp.floor(jnp.log2(largest)) + 1.0, -100.0, 100.0)


def to_codes(values, exponent):
    return jnp.round(values * (jnp.exp2(-exponent) * FULL)).astype(jnp.int32).astype(jnp.int16)


def write_pieces(load, count, payload_ref):
    row = lax.broadcasted_iota(jnp.int32, (SCALE_ROWS, HALF), 0)
    scales = jnp.zeros((SCALE_ROWS, HALF), jnp.float32)
    for k in range(count):
        values = load(k)
        exponent = exponent_of(jnp.max(jnp.abs(values), axis=0, keepdims=True))
        payload_ref[k * PIECE : (k + 1) * PIECE, :] = to_codes(values, exponent)
        scales = jnp.where(row == k, exponent, scales)
    payload_ref[count * PIECE :, :] = scales.astype(jnp.int32).astype(jnp.int16)


def read_scales(payload_ref, count):
    exponents = payload_ref[count * PIECE :, :].astype(jnp.int32).astype(jnp.float32)
    return jnp.exp2(exponents) * (1.0 / FULL)


def read_piece(payload_ref, scales, k):
    codes = payload_ref[k * PIECE : (k + 1) * PIECE, :].astype(jnp.int32).astype(jnp.float32)
    return codes * scales[k : k + 1, :]


def place_in_order():
    core = lax.axis_index("core")

    def order(v):
        first = jnp.where(core == 0, v ^ 1, 3 - v)
        second = lambda u: jnp.where(core == 0, 3 - u, u ^ 1)
        return [v, second(v), first, second(first)]

    return core, order(lax.axis_index("x")), order(lax.axis_index("y"))


def load_rows(given, scratch, staged):
    fitted_ref, table_ref, sizes_ref = given
    mask_ref, same_ref, cross_ref = scratch
    core = lax.axis_index("core")
    blocks = table_ref.shape[0]
    live = lambda b, r: sizes_ref[b, TILES] > r
    copies = []
    if staged is not None:
        for q in range(blocks * AUX_PER_BLOCK):
            copies.append(pltpu.make_async_copy(fitted_ref.at[q], staged[0].at[q], staged[1].at[q]))

            @pl.when(live(q // AUX_PER_BLOCK, q % AUX_PER_BLOCK))
            def _(q=q):
                copies[q].start()

        fitted_ref = staged[0]
    tile = lax.broadcasted_iota(jnp.int32, (16, 2 * HALF), 0)
    column = lax.broadcasted_iota(jnp.int32, (16, 2 * HALF), 1)
    spread = (column // BASIS_PER_TILE == tile).astype(jnp.bfloat16)
    mask_ref[...] = jnp.dot(
        table_ref[:, :TILES].astype(jnp.float32).astype(jnp.bfloat16), spread, preferred_element_type=jnp.float32
    )
    first = jnp.int32(0)
    for b in range(blocks):
        for r in range(AUX_PER_BLOCK):

            @pl.when(live(b, r))
            def _(b=b, r=r, slot=first + r):
                q = b * AUX_PER_BLOCK + r
                if copies:
                    copies[q].wait()
                rows = pl.ds(pl.multiple_of(slot * 48, 16), 48)
                for j in range(8):
                    for out_ref, parity in ((same_ref, core), (cross_ref, 1 - core)):
                        lanes = pl.ds(pl.multiple_of((2 * j + parity) * 128, 128), 128)
                        mask = mask_ref[b : b + 1, lanes].astype(jnp.bfloat16)
                        out_ref[rows, j * 128 : (j + 1) * 128] = fitted_ref[q, :, lanes] * mask

        first = first + sizes_ref[b, TILES]
    chunks = jnp.maximum((first * 48 + 255) // 256, 4)

    def clear(i, carry):
        rows = pl.ds(pl.multiple_of(i * 16, 16), 16)
        same_ref[rows, :] = jnp.zeros((16, HALF), jnp.bfloat16)
        cross_ref[rows, :] = jnp.zeros((16, HALF), jnp.bfloat16)
        return carry

    lax.fori_loop(first * 3, chunks * 16, clear, 0)
    return chunks


def over_depths(chunks, body):
    for depth in (4, 5, 6):

        @pl.when(chunks == depth)
        def _(depth=depth):
            body(depth * 256)


def product(left, right):
    return lax.dot_general(left, right, (((0,), (0,)), ((), ())), preferred_element_type=jnp.float32)


def place(values, x, out_ref, columns):
    for zh in range(2):
        for zl in range(4):
            for y in range(4):
                source = zh * 128 + zl * 32 + y * 8
                target = (zh * 4 + zl) * 8
                out_ref[x * 4 + y, target : target + 8, columns] = values[source : source + 8, :]


def own_kernel(*refs):
    given, (x_ref, y_ref), scratch, staged = refs[:3], refs[3:5], refs[5:8], refs[8:10]
    same_ref, cross_ref = scratch[1:3]

    def body(depth):
        for x in range(4):
            rows = slice(x * 256, (x + 1) * 256)
            x_ref[rows, x * 256 :] = product(same_ref[:depth, rows], same_ref[:depth, x * 256 :])
        for x in range(4):
            rows = slice(x * 256, (x + 1) * 256)
            y_ref[rows, :] = product(same_ref[:depth, rows], cross_ref[:depth, :])

    over_depths(load_rows(given, scratch, staged), body)


def send_half(total_ref, slots, state_ref, payload_ref):
    for k in range(8):
        state_ref[k] = total_ref[slots[k]]
    write_pieces(lambda k: total_ref[slots[8 + k]], 8, payload_ref)


def other_kernel(*refs):
    given, (own_x, own_y), scratch = refs[:3], refs[3:5], refs[9:12]
    state_x, payload_x, state_y, payload_y, total_ref = *refs[5:9], refs[12]
    same_ref, cross_ref = scratch[1:3]
    chunks = load_rows(given, scratch, None)
    _, xs, ys = place_in_order()

    def same(depth):
        for x in range(4):
            rows = slice(x * 256, (x + 1) * 256)
            result = product(same_ref[:depth, rows], same_ref[:depth, x * 256 :]) + own_x[rows, x * 256 :]
            place(result, x, total_ref, slice(x * 256, HALF))
            for right in range(x + 1, 4):
                block = result[:, (right - x) * 256 : (right - x + 1) * 256]
                place(block.T, right, total_ref, rows)

    def cross(depth):
        for x in range(4):
            rows = slice(x * 256, (x + 1) * 256)
            result = product(same_ref[:depth, rows], cross_ref[:depth, :]) + own_y[rows, :]
            place(result, x, total_ref, slice(0, HALF))

    over_depths(chunks, same)
    send_half(total_ref, [x * 4 + y for x in xs for y in ys], state_x, payload_x)
    over_depths(chunks, cross)
    send_half(total_ref, [x * 4 + y for y in ys for x in xs], state_y, payload_y)


def step_kernel(count, state_ref, got_ref, next_ref, payload_ref):
    scales = read_scales(got_ref, count)
    half = count // 2
    for k in range(half):
        next_ref[k] = state_ref[k] + read_piece(got_ref, scales, k)
    write_pieces(lambda k: state_ref[half + k] + read_piece(got_ref, scales, half + k), half, payload_ref)


def pack_kernel(state_x, got_x, state_y, got_y, out_ref):
    sums = [
        state_ref[0] + read_piece(got_ref, read_scales(got_ref, 1), 0)
        for state_ref, got_ref in ((state_x, got_x), (state_y, got_y))
    ]
    lane = lax.broadcasted_iota(jnp.int32, (16, 128), 1)
    for z in range(8):
        rows = jnp.concatenate([s[z * 8 : (z + 1) * 8, :] for s in sums], axis=0)
        exponents = jnp.zeros((16, 128), jnp.float32)
        for g in range(8):
            values = rows[:, g * 128 : (g + 1) * 128]
            exponent = exponent_of(jnp.max(jnp.abs(values), axis=1, keepdims=True))
            out_ref[z, :, g * 128 : (g + 1) * 128] = to_codes(values, exponent)
            exponents = jnp.where(lane == g, exponent, exponents)
        out_ref[z, :, HALF:] = exponents.astype(jnp.int32).astype(jnp.int16)


def unpack_kernel(got_ref, out_ref):
    total = [jnp.zeros((16, 128), jnp.float32) for _ in range(8)]
    for z in range(8):
        scales = jnp.exp2(got_ref[z, :, HALF:].astype(jnp.int32).astype(jnp.float32)) * (1.0 / FULL)
        for g in range(8):
            codes = got_ref[z, :, g * 128 : (g + 1) * 128].astype(jnp.int32).astype(jnp.float32)
            total[g] = total[g] + codes * scales[:, g : g + 1]
    core = lax.axis_index("core")
    for g in range(8):
        for rows, parity in ((total[g][:8], core), (total[g][8:], 1 - core)):
            out_ref[:, pl.ds(pl.multiple_of((2 * g + parity) * 128, 128), 128)] = rows


VMEM = pl.BlockSpec(memory_space=pltpu.VMEM)
ANY = pl.BlockSpec(memory_space=pl.ANY)
SMEM = pl.BlockSpec(memory_space=pltpu.SMEM)


def call(kernel, inputs, outputs, limit, scratch=(), flops=0, spaces=()):
    moved = sum(int(np.prod(a.shape)) * a.dtype.itemsize for a in (*inputs, *outputs))
    return pl.pallas_call(
        kernel,
        in_specs=[*spaces, *[VMEM] * (len(inputs) - len(spaces))],
        out_specs=[VMEM] * len(outputs),
        out_shape=list(outputs),
        scratch_shapes=list(scratch),
        compiler_params=pltpu.CompilerParams(vmem_limit_bytes=limit << 20),
        cost_estimate=pl.CostEstimate(flops=flops, bytes_accessed=moved, transcendentals=0),
    )(*inputs)


def state_shape(count):
    return jax.ShapeDtypeStruct((count, PIECE, HALF), jnp.float32)


def payload_shape(count):
    return jax.ShapeDtypeStruct((count * PIECE + SCALE_ROWS, HALF), jnp.int16)


def on_device(fitted, screen, block_sizes):
    rows = fitted.shape[0]
    table = jnp.concatenate([screen, block_sizes[:, None]], axis=1)
    other, other_table = swap(fitted, "core"), swap(table, "core")
    square = jax.ShapeDtypeStruct((HALF, HALF), jnp.float32)
    packed = pltpu.VMEM((rows * 48, HALF), jnp.bfloat16)
    scratch = (pltpu.VMEM((screen.shape[0], 2 * HALF), jnp.float32), packed, packed)
    staged = (pltpu.VMEM(fitted.shape, jnp.bfloat16), pltpu.SemaphoreType.DMA((rows,)))
    work = 3 * rows * 48 * HALF * HALF
    own = call(own_kernel, (fitted, table, table), (square, square), OWN_LIMIT, (*scratch, *staged), work, (ANY, VMEM, SMEM))
    state_x, payload_x, state_y, payload_y = call(
        other_kernel,
        (other, other_table, other_table, *own),
        (state_shape(8), payload_shape(8)) * 2,
        OTHER_LIMIT,
        (*scratch, pltpu.VMEM((16, PIECE, HALF), jnp.float32)),
        work,
        (VMEM, VMEM, SMEM),
    )
    streams = [(state_x, payload_x), (state_y, payload_y)]
    got = [swap(payload, step) for (_, payload), step in zip(streams, ("x1", "y1"))]
    for steps, count in ((("x2", "y2"), 8), (("y1", "x1"), 4), (("y2", "x2"), 2)):
        streams = [
            call(
                functools.partial(step_kernel, count),
                (state, payload),
                (state_shape(count // 2), payload_shape(count // 2)),
                8,
            )
            for (state, _), payload in zip(streams, got)
        ]
        got = [swap(payload, step) for (_, payload), step in zip(streams, steps)]
    message = call(
        pack_kernel,
        (streams[0][0], got[0], streams[1][0], got[1]),
        (jax.ShapeDtypeStruct((8, 16, HALF + 128), jnp.int16),),
        4,
    )[0]
    message = lax.all_to_all(message, ("zh", "zl"), 0, 0, tiled=True)
    return call(unpack_kernel, (message,), (jax.ShapeDtypeStruct((8, 2 * HALF), jnp.float32),), 4)[0]


def solution(mesh):
    physical = Mesh(mesh.devices.reshape(SIZES), AXES)
    return jax.shard_map(
        on_device,
        mesh=physical,
        in_specs=(P(("x", "zh", "core"), ("zl", "y"), None), P(("x", "zh", "core"), None), P(("x", "zh", "core"))),
        out_specs=P(AXES, None),
        check_vma=False,
    )
```

```python
import functools

import jax
import jax.numpy as jnp
import numpy as np
from jax import lax
from jax.experimental import pallas as pl
from jax.experimental.pallas import tpu as pltpu
from jax.sharding import Mesh, PartitionSpec as P

AUX_PER_BLOCK = 4
BASIS_PER_TILE = 128
TILES = 16
SIZES = (4, 2, 2, 4, 4)
AXES = ("x", "zh", "core", "zl", "y")
FULL = 32767.0
HALF = 1024
PIECE = 64
PART = 512
OWN_LIMIT = 42
OTHER_LIMIT = 19
SCALE_ROWS = 16


def partner_a(v, core):
    return v ^ 1 if core == 0 else 3 - v


def partner_b(v, core):
    return 3 - v if core == 0 else v ^ 1


PARTNERS = {
    "core": lambda x, y, core: (x, y, 1 - core),
    "x1": lambda x, y, core: (partner_a(x, core), y, core),
    "x2": lambda x, y, core: (partner_b(x, core), y, core),
    "y1": lambda x, y, core: (x, partner_a(y, core), core),
    "y2": lambda x, y, core: (x, partner_b(y, core), core),
    **{f"x+{k}": (lambda x, y, core, k=k: ((x + k) % 4, y, core)) for k in (1, 2, 3)},
    **{f"y+{k}": (lambda x, y, core, k=k: (x, (y + k) % 4, core)) for k in (1, 2, 3)},
}


def swap(value, step):
    pairs = []
    for here in range(256):
        x, zh, core, zl, y = (int(v) for v in np.unravel_index(here, SIZES))
        to_x, to_y, to_core = PARTNERS[step](x, y, core)
        pairs.append((here, int(np.ravel_multi_index((to_x, zh, to_core, zl, to_y), SIZES))))
    return lax.ppermute(value, AXES, pairs)


def exponent_of(largest):
    return jnp.clip(jnp.floor(jnp.log2(largest)) + 1.0, -100.0, 100.0)


def to_codes(values, exponent):
    return jnp.round(values * (jnp.exp2(-exponent) * FULL)).astype(jnp.int32).astype(jnp.int16)


def write_pieces(load, count, payload_ref, columns=slice(None)):
    scales = None
    for k in range(count):
        values = load(k)
        if scales is None:
            row = lax.broadcasted_iota(jnp.int32, (SCALE_ROWS, values.shape[1]), 0)
            scales = jnp.zeros(row.shape, jnp.float32)
        exponent = exponent_of(jnp.max(jnp.abs(values), axis=0, keepdims=True))
        payload_ref[k * PIECE : (k + 1) * PIECE, columns] = to_codes(values, exponent)
        scales = jnp.where(row == k, exponent, scales)
    payload_ref[count * PIECE :, columns] = scales.astype(jnp.int32).astype(jnp.int16)


def read_scales(payload_ref, count):
    exponents = payload_ref[count * PIECE :, :].astype(jnp.int32).astype(jnp.float32)
    return jnp.exp2(exponents) * (1.0 / FULL)


def read_piece(payload_ref, scales, k):
    codes = payload_ref[k * PIECE : (k + 1) * PIECE, :].astype(jnp.int32).astype(jnp.float32)
    return codes * scales[k : k + 1, :]


def place_in_order():
    core = lax.axis_index("core")

    def order(v):
        first = jnp.where(core == 0, v ^ 1, 3 - v)
        second = lambda u: jnp.where(core == 0, 3 - u, u ^ 1)
        return [v, second(v), first, second(first)]

    return core, order(lax.axis_index("x")), order(lax.axis_index("y"))


def load_rows(given, scratch, staged):
    fitted_ref, table_ref, sizes_ref = given
    mask_ref, same_ref, cross_ref = scratch
    core = lax.axis_index("core")
    blocks = table_ref.shape[0]
    live = lambda b, r: sizes_ref[b, TILES] > r
    copies = []
    if staged is not None:
        for q in range(blocks * AUX_PER_BLOCK):
            copies.append(pltpu.make_async_copy(fitted_ref.at[q], staged[0].at[q], staged[1].at[q]))

            @pl.when(live(q // AUX_PER_BLOCK, q % AUX_PER_BLOCK))
            def _(q=q):
                copies[q].start()

        fitted_ref = staged[0]
    tile = lax.broadcasted_iota(jnp.int32, (16, 2 * HALF), 0)
    column = lax.broadcasted_iota(jnp.int32, (16, 2 * HALF), 1)
    spread = (column // BASIS_PER_TILE == tile).astype(jnp.bfloat16)
    mask_ref[...] = jnp.dot(
        table_ref[:, :TILES].astype(jnp.float32).astype(jnp.bfloat16), spread, preferred_element_type=jnp.float32
    )
    first = jnp.int32(0)
    for b in range(blocks):
        for r in range(AUX_PER_BLOCK):

            @pl.when(live(b, r))
            def _(b=b, r=r, slot=first + r):
                q = b * AUX_PER_BLOCK + r
                if copies:
                    copies[q].wait()
                rows = pl.ds(pl.multiple_of(slot * 48, 16), 48)
                for j in range(8):
                    for out_ref, parity in ((same_ref, core), (cross_ref, 1 - core)):
                        lanes = pl.ds(pl.multiple_of((2 * j + parity) * 128, 128), 128)
                        mask = mask_ref[b : b + 1, lanes].astype(jnp.bfloat16)
                        out_ref[rows, j * 128 : (j + 1) * 128] = fitted_ref[q, :, lanes] * mask

        first = first + sizes_ref[b, TILES]
    chunks = chunks_of(first)

    def clear(i, carry):
        rows = pl.ds(pl.multiple_of(i * 16, 16), 16)
        same_ref[rows, :] = jnp.zeros((16, HALF), jnp.bfloat16)
        cross_ref[rows, :] = jnp.zeros((16, HALF), jnp.bfloat16)
        return carry

    lax.fori_loop(first * 3, chunks * 16, clear, 0)
    return chunks


def chunks_of(live_rows):
    return jnp.maximum((live_rows * 48 + 255) // 256, 4)


def over_depths(chunks, body):
    for depth in (4, 5, 6):

        @pl.when(chunks == depth)
        def _(depth=depth):
            body(depth * 256)


def product(left, right):
    return lax.dot_general(left, right, (((0,), (0,)), ((), ())), preferred_element_type=jnp.float32)


def place(values, x, out_ref, columns):
    for zh in range(2):
        for zl in range(4):
            for y in range(4):
                source = zh * 128 + zl * 32 + y * 8
                target = (zh * 4 + zl) * 8
                out_ref[x * 4 + y, target : target + 8, columns] = values[source : source + 8, :]


def own_kernel(*refs):
    given, (x_ref, y_ref), scratch, staged = refs[:3], refs[3:5], refs[5:8], refs[8:10]
    same_ref, cross_ref = scratch[1:3]

    def body(depth):
        for x in range(4):
            rows = slice(x * 256, (x + 1) * 256)
            x_ref[rows, x * 256 :] = product(same_ref[:depth, rows], same_ref[:depth, x * 256 :])
        for x in range(4):
            rows = slice(x * 256, (x + 1) * 256)
            y_ref[rows, :] = product(same_ref[:depth, rows], cross_ref[:depth, :])

    over_depths(load_rows(given, scratch, staged), body)


def send_half(total_ref, slots, state_ref, payload_ref):
    for k in range(8):
        state_ref[k] = total_ref[slots[k]]
    write_pieces(lambda k: total_ref[slots[8 + k]], 8, payload_ref)


def slot_orders():
    _, xs, ys = place_in_order()
    turned = lambda v: [(v + k) % 4 for k in range(4)]
    return [x * 4 + y for x in xs for y in turned(ys[0])], [x * 4 + y for y in ys for x in turned(xs[0])]


def cross_part(same_ref, cross_ref, own_ref, total_ref, part, depth):
    columns = slice(part * PART, (part + 1) * PART)
    for x in range(4):
        rows = slice(x * 256, (x + 1) * 256)
        result = product(same_ref[:depth, rows], cross_ref[:depth, columns]) + own_ref[rows, columns]
        place(result, x, total_ref, slice(None))


def left_kernel(
    fitted_ref, table_ref, sizes_ref, own_x, own_y,
    state_x, payload_x, state_y, payload_y, same_ref, cross_ref, upper_ref, mask_ref, total_ref,
):
    chunks = load_rows((fitted_ref, table_ref, sizes_ref), (mask_ref, same_ref, cross_ref), None)
    x_slots, y_slots = slot_orders()

    def same(depth):
        for x in range(2):
            rows = slice(x * 256, (x + 1) * 256)
            result = product(same_ref[:depth, rows], same_ref[:depth, x * 256 :]) + own_x[rows, x * 256 :]
            upper_ref[rows, :] = result[:, -PART:]
            place(result[:, : PART - x * 256], x, total_ref, slice(x * 256, PART))
            for right in range(x + 1, 4):
                block = result[:, (right - x) * 256 : (right - x + 1) * 256]
                place(block.T, right, total_ref, rows)

    over_depths(chunks, same)
    send_half(total_ref, x_slots, state_x, payload_x)
    over_depths(chunks, functools.partial(cross_part, same_ref, cross_ref, own_y, total_ref, 0))
    send_half(total_ref, y_slots, state_y, payload_y)


def right_kernel(
    sizes_ref, same_ref, cross_ref, upper_ref, own_x, own_y,
    state_x, payload_x, state_y, payload_y, total_ref,
):
    live_rows = sizes_ref[0, TILES]
    for b in range(1, sizes_ref.shape[0]):
        live_rows = live_rows + sizes_ref[b, TILES]
    chunks = chunks_of(live_rows)
    x_slots, y_slots = slot_orders()

    def same(depth):
        for x in range(2):
            place(upper_ref[x * 256 : (x + 1) * 256, :], x, total_ref, slice(None))
        for x in range(2, 4):
            rows = slice(x * 256, (x + 1) * 256)
            result = product(same_ref[:depth, rows], same_ref[:depth, x * 256 :]) + own_x[rows, x * 256 :]
            place(result, x, total_ref, slice((x - 2) * 256, PART))
            if x == 2:
                place(result[:, 256:].T, 3, total_ref, slice(0, 256))

    over_depths(chunks, same)
    send_half(total_ref, x_slots, state_x, payload_x)
    over_depths(chunks, functools.partial(cross_part, same_ref, cross_ref, own_y, total_ref, 1))
    send_half(total_ref, y_slots, state_y, payload_y)


def step_kernel(count, parts, *refs):
    next_ref, payload_ref = refs[2 * parts :]
    half = count // 2
    for part in range(parts):
        state_ref, got_ref = refs[2 * part : 2 * part + 2]
        width = state_ref.shape[2]
        columns = slice(part * width, (part + 1) * width)
        scales = read_scales(got_ref, count)
        for k in range(half):
            next_ref[k, :, columns] = state_ref[k] + read_piece(got_ref, scales, k)

        def load(k, state_ref=state_ref, got_ref=got_ref, scales=scales):
            return state_ref[half + k] + read_piece(got_ref, scales, half + k)

        write_pieces(load, half, payload_ref, columns)


def spread_kernel(parts, *refs):
    next_ref, *payloads = refs[2 * parts :]
    for part in range(parts):
        state_ref, got_ref = refs[2 * part : 2 * part + 2]
        width = state_ref.shape[2]
        columns = slice(part * width, (part + 1) * width)
        scales = read_scales(got_ref, 4)
        next_ref[0, :, columns] = state_ref[0] + read_piece(got_ref, scales, 0)
        for k in range(1, 4):
            piece = state_ref[k] + read_piece(got_ref, scales, k)
            write_pieces(lambda _, piece=piece: piece, 1, payloads[k - 1], columns)


def pack_kernel(*refs):
    *streams, out_ref = refs
    sums = []
    for state_ref, *got in (streams[:4], streams[4:]):
        total = state_ref[0]
        for got_ref in got:
            total = total + read_piece(got_ref, read_scales(got_ref, 1), 0)
        sums.append(total)
    lane = lax.broadcasted_iota(jnp.int32, (16, 128), 1)
    for z in range(8):
        rows = jnp.concatenate([s[z * 8 : (z + 1) * 8, :] for s in sums], axis=0)
        exponents = jnp.zeros((16, 128), jnp.float32)
        for g in range(8):
            values = rows[:, g * 128 : (g + 1) * 128]
            exponent = exponent_of(jnp.max(jnp.abs(values), axis=1, keepdims=True))
            out_ref[z, :, g * 128 : (g + 1) * 128] = to_codes(values, exponent)
            exponents = jnp.where(lane == g, exponent, exponents)
        out_ref[z, :, HALF:] = exponents.astype(jnp.int32).astype(jnp.int16)


def unpack_kernel(got_ref, out_ref):
    total = [jnp.zeros((16, 128), jnp.float32) for _ in range(8)]
    for z in range(8):
        scales = jnp.exp2(got_ref[z, :, HALF:].astype(jnp.int32).astype(jnp.float32)) * (1.0 / FULL)
        for g in range(8):
            codes = got_ref[z, :, g * 128 : (g + 1) * 128].astype(jnp.int32).astype(jnp.float32)
            total[g] = total[g] + codes * scales[:, g : g + 1]
    core = lax.axis_index("core")
    for g in range(8):
        for rows, parity in ((total[g][:8], core), (total[g][8:], 1 - core)):
            out_ref[:, pl.ds(pl.multiple_of((2 * g + parity) * 128, 128), 128)] = rows


VMEM = pl.BlockSpec(memory_space=pltpu.VMEM)
ANY = pl.BlockSpec(memory_space=pl.ANY)
SMEM = pl.BlockSpec(memory_space=pltpu.SMEM)


def call(kernel, inputs, outputs, limit, scratch=(), flops=0, spaces=()):
    moved = sum(int(np.prod(a.shape)) * a.dtype.itemsize for a in (*inputs, *outputs))
    return pl.pallas_call(
        kernel,
        in_specs=[*spaces, *[VMEM] * (len(inputs) - len(spaces))],
        out_specs=[VMEM] * len(outputs),
        out_shape=list(outputs),
        scratch_shapes=list(scratch),
        compiler_params=pltpu.CompilerParams(vmem_limit_bytes=limit << 20),
        cost_estimate=pl.CostEstimate(flops=flops, bytes_accessed=moved, transcendentals=0),
    )(*inputs)


def state_shape(count, width):
    return jax.ShapeDtypeStruct((count, PIECE, width), jnp.float32)


def payload_shape(count, width):
    return jax.ShapeDtypeStruct((count * PIECE + SCALE_ROWS, width), jnp.int16)


def on_device(fitted, screen, block_sizes):
    rows = fitted.shape[0]
    table = jnp.concatenate([screen, block_sizes[:, None]], axis=1)
    other, other_table = swap(fitted, "core"), swap(table, "core")
    square = jax.ShapeDtypeStruct((HALF, HALF), jnp.float32)
    packed = pltpu.VMEM((rows * 48, HALF), jnp.bfloat16)
    mask = pltpu.VMEM((screen.shape[0], 2 * HALF), jnp.float32)
    staged = (pltpu.VMEM(fitted.shape, jnp.bfloat16), pltpu.SemaphoreType.DMA((rows,)))
    total = pltpu.VMEM((16, PIECE, PART), jnp.float32)
    work = 3 * rows * 48 * HALF * HALF
    own = call(
        own_kernel, (fitted, table, table), (square, square), OWN_LIMIT, (mask, packed, packed, *staged), work, (ANY, VMEM, SMEM)
    )
    part = (state_shape(8, PART), payload_shape(8, PART)) * 2
    half = jax.ShapeDtypeStruct((rows * 48, HALF), jnp.bfloat16)
    upper = jax.ShapeDtypeStruct((PART, PART), jnp.float32)
    *left, same, cross, upper = call(
        left_kernel,
        (other, other_table, other_table, *own),
        (*part, half, half, upper),
        OTHER_LIMIT,
        (mask, total),
        work // 2,
        (VMEM, VMEM, SMEM),
    )
    right = call(
        right_kernel, (other_table, same, cross, upper, *own), part, OTHER_LIMIT, (total,), work // 2, (SMEM,)
    )
    states = [left[0], left[2], right[0], right[2]]
    got = [swap(p, step) for p, step in zip((left[1], left[3], right[1], right[3]), ("x1", "y1", "x1", "y1"))]

    def advance(count, width, pairs, step):
        state, payload = call(
            functools.partial(step_kernel, count, len(pairs)),
            tuple(a for pair in pairs for a in pair),
            (state_shape(count // 2, width), payload_shape(count // 2, width)),
            10,
        )
        return state, swap(payload, step)

    moved = [advance(8, PART, [pair], step) for pair, step in zip(zip(states[:2], got[:2]), ("x2", "y2"))]
    *tied, first, second = lax.optimization_barrier((states[2], states[3], moved[0][1], moved[1][1]))
    moved = [(moved[0][0], first), (moved[1][0], second)]
    moved += [advance(8, PART, [pair], step) for pair, step in zip(zip(tied, got[2:]), ("x2", "y2"))]
    streams = []
    for i, axis in enumerate("yx"):
        state, *payloads = call(
            functools.partial(spread_kernel, 2),
            (*moved[i], *moved[i + 2]),
            (state_shape(1, HALF), *[payload_shape(1, HALF)] * 3),
            10,
        )
        streams += [state, *(swap(p, f"{axis}+{k}") for k, p in enumerate(payloads, 1))]
    message = call(
        pack_kernel,
        streams,
        (jax.ShapeDtypeStruct((8, 16, HALF + 128), jnp.int16),),
        4,
    )[0]
    message = lax.all_to_all(message, ("zh", "zl"), 0, 0, tiled=True)
    return call(unpack_kernel, (message,), (jax.ShapeDtypeStruct((8, 2 * HALF), jnp.float32),), 4)[0]


def solution(mesh):
    physical = Mesh(mesh.devices.reshape(SIZES), AXES)
    return jax.shard_map(
        on_device,
        mesh=physical,
        in_specs=(P(("x", "zh", "core"), ("zl", "y"), None), P(("x", "zh", "core"), None), P(("x", "zh", "core"))),
        out_specs=P(AXES, None),
        check_vma=False,
    )
```

```python
import functools

import jax
import jax.numpy as jnp
import numpy as np
from jax import lax
from jax.experimental import pallas as pl
from jax.experimental.pallas import tpu as pltpu
from jax.sharding import Mesh, PartitionSpec as P

AUX_PER_BLOCK = 4
BASIS_PER_TILE = 128
TILES = 16
SIZES = (4, 2, 2, 4, 4)
AXES = ("x", "zh", "core", "zl", "y")
FULL = 32767.0
HALF = 1024
PIECE = 64
PART = 512
OWN_LIMIT = 42
OTHER_LIMIT = 19
SCALE_ROWS = 16


def partner_a(v, core):
    return v ^ 1 if core == 0 else 3 - v


def partner_b(v, core):
    return 3 - v if core == 0 else v ^ 1


PARTNERS = {
    "core": lambda x, y, core: (x, y, 1 - core),
    "x1": lambda x, y, core: (partner_a(x, core), y, core),
    "x2": lambda x, y, core: (partner_b(x, core), y, core),
    "y1": lambda x, y, core: (x, partner_a(y, core), core),
    "y2": lambda x, y, core: (x, partner_b(y, core), core),
    **{f"x+{k}": (lambda x, y, core, k=k: ((x + k) % 4, y, core)) for k in (1, 2, 3)},
    **{f"y+{k}": (lambda x, y, core, k=k: (x, (y + k) % 4, core)) for k in (1, 2, 3)},
}


def swap(value, step):
    pairs = []
    for here in range(256):
        x, zh, core, zl, y = (int(v) for v in np.unravel_index(here, SIZES))
        to_x, to_y, to_core = PARTNERS[step](x, y, core)
        pairs.append((here, int(np.ravel_multi_index((to_x, zh, to_core, zl, to_y), SIZES))))
    return lax.ppermute(value, AXES, pairs)


def exponent_of(largest):
    return jnp.clip(jnp.floor(jnp.log2(largest)) + 1.0, -100.0, 100.0)


def to_codes(values, exponent):
    return jnp.round(values * (jnp.exp2(-exponent) * FULL)).astype(jnp.int32).astype(jnp.int16)


def write_pieces(load, count, payload_ref, columns=slice(None)):
    scales = None
    for k in range(count):
        values = load(k)
        if scales is None:
            row = lax.broadcasted_iota(jnp.int32, (SCALE_ROWS, values.shape[1]), 0)
            scales = jnp.zeros(row.shape, jnp.float32)
        exponent = exponent_of(jnp.max(jnp.abs(values), axis=0, keepdims=True))
        payload_ref[k * PIECE : (k + 1) * PIECE, columns] = to_codes(values, exponent)
        scales = jnp.where(row == k, exponent, scales)
    payload_ref[count * PIECE :, columns] = scales.astype(jnp.int32).astype(jnp.int16)


def read_scales(payload_ref, count):
    exponents = payload_ref[count * PIECE :, :].astype(jnp.int32).astype(jnp.float32)
    return jnp.exp2(exponents) * (1.0 / FULL)


def read_piece(payload_ref, scales, k):
    codes = payload_ref[k * PIECE : (k + 1) * PIECE, :].astype(jnp.int32).astype(jnp.float32)
    return codes * scales[k : k + 1, :]


def place_in_order():
    core = lax.axis_index("core")

    def order(v):
        first = jnp.where(core == 0, v ^ 1, 3 - v)
        second = lambda u: jnp.where(core == 0, 3 - u, u ^ 1)
        return [v, second(v), first, second(first)]

    return core, order(lax.axis_index("x")), order(lax.axis_index("y"))


def load_rows(given, scratch, staged):
    fitted_ref, table_ref, sizes_ref = given
    mask_ref, same_ref, cross_ref = scratch
    core = lax.axis_index("core")
    blocks = table_ref.shape[0]
    live = lambda b, r: sizes_ref[b, TILES] > r

    def copy_of(q):
        return pltpu.make_async_copy(fitted_ref.at[q], staged[0].at[q], staged[1].at[q])

    def fetch(b, carry):
        for r in range(AUX_PER_BLOCK):

            @pl.when(live(b, r))
            def _(r=r):
                copy_of(b * AUX_PER_BLOCK + r).start()

        return carry

    if staged is not None:
        lax.fori_loop(0, blocks, fetch, 0)
    tile = lax.broadcasted_iota(jnp.int32, (16, 2 * HALF), 0)
    column = lax.broadcasted_iota(jnp.int32, (16, 2 * HALF), 1)
    spread = (column // BASIS_PER_TILE == tile).astype(jnp.bfloat16)
    mask = jnp.dot(
        table_ref[:, :TILES].astype(jnp.float32).astype(jnp.bfloat16), spread, preferred_element_type=jnp.float32
    )
    for b in range(blocks):
        mask_ref[b] = mask[b : b + 1, :]
    rows_ref = fitted_ref if staged is None else staged[0]

    def pack(b, first):
        for r in range(AUX_PER_BLOCK):

            @pl.when(live(b, r))
            def _(r=r):
                q = b * AUX_PER_BLOCK + r
                if staged is not None:
                    copy_of(q).wait()
                rows = pl.ds(pl.multiple_of((first + r) * 48, 16), 48)
                for j in range(8):
                    for out_ref, parity in ((same_ref, core), (cross_ref, 1 - core)):
                        lanes = pl.ds(pl.multiple_of((2 * j + parity) * 128, 128), 128)
                        keep = mask_ref[b, :, lanes].astype(jnp.bfloat16)
                        out_ref[rows, j * 128 : (j + 1) * 128] = rows_ref[q, :, lanes] * keep

        return first + sizes_ref[b, TILES]

    first = lax.fori_loop(0, blocks, pack, jnp.int32(0))
    chunks = chunks_of(first)

    def clear(i, carry):
        rows = pl.ds(pl.multiple_of(i * 16, 16), 16)
        same_ref[rows, :] = jnp.zeros((16, HALF), jnp.bfloat16)
        cross_ref[rows, :] = jnp.zeros((16, HALF), jnp.bfloat16)
        return carry

    lax.fori_loop(first * 3, chunks * 16, clear, 0)
    return chunks


def chunks_of(live_rows):
    return jnp.maximum((live_rows * 48 + 255) // 256, 5)


def over_depths(chunks, body):
    for depth in (5, 6):

        @pl.when(chunks == depth)
        def _(depth=depth):
            body(depth * 256)


def product(left, right):
    return lax.dot_general(left, right, (((0,), (0,)), ((), ())), preferred_element_type=jnp.float32)


def place(values, x, out_ref, columns):
    for zh in range(2):
        for zl in range(4):
            for y in range(4):
                source = zh * 128 + zl * 32 + y * 8
                target = (zh * 4 + zl) * 8
                out_ref[x * 4 + y, target : target + 8, columns] = values[source : source + 8, :]


def own_kernel(*refs):
    given, (x_ref, y_ref), scratch, staged = refs[:3], refs[3:5], refs[5:8], refs[8:10]
    same_ref, cross_ref = scratch[1:3]

    def body(depth):
        for x in range(4):
            rows = slice(x * 256, (x + 1) * 256)
            x_ref[rows, x * 256 :] = product(same_ref[:depth, rows], same_ref[:depth, x * 256 :])

        def cross(x, carry):
            rows = pl.ds(pl.multiple_of(x * 256, 256), 256)
            y_ref[rows, :] = product(same_ref[:depth, rows], cross_ref[:depth, :])
            return carry

        lax.fori_loop(0, 4, cross, 0)

    over_depths(load_rows(given, scratch, staged), body)


def send_half(total_ref, slots, state_ref, payload_ref):
    for k in range(8):
        state_ref[k] = total_ref[slots[k]]
    write_pieces(lambda k: total_ref[slots[8 + k]], 8, payload_ref)


def slot_orders():
    _, xs, ys = place_in_order()
    turned = lambda v: [(v + k) % 4 for k in range(4)]
    return [x * 4 + y for x in xs for y in turned(ys[0])], [x * 4 + y for y in ys for x in turned(xs[0])]


def cross_part(same_ref, cross_ref, own_ref, total_ref, part, depth):
    columns = slice(part * PART, (part + 1) * PART)

    def body(x, carry):
        rows = pl.ds(pl.multiple_of(x * 256, 256), 256)
        result = product(same_ref[:depth, rows], cross_ref[:depth, columns]) + own_ref[rows, columns]
        place(result, x, total_ref, slice(None))
        return carry

    lax.fori_loop(0, 4, body, 0)


def left_kernel(
    fitted_ref, table_ref, sizes_ref, own_x, own_y,
    state_x, payload_x, state_y, payload_y, same_ref, cross_ref, upper_ref, mask_ref, total_ref,
):
    chunks = load_rows((fitted_ref, table_ref, sizes_ref), (mask_ref, same_ref, cross_ref), None)
    x_slots, y_slots = slot_orders()

    def same(depth):
        for x in range(2):
            rows = slice(x * 256, (x + 1) * 256)
            result = product(same_ref[:depth, rows], same_ref[:depth, x * 256 :]) + own_x[rows, x * 256 :]
            upper_ref[rows, :] = result[:, -PART:]
            place(result[:, : PART - x * 256], x, total_ref, slice(x * 256, PART))
            for right in range(x + 1, 4):
                block = result[:, (right - x) * 256 : (right - x + 1) * 256]
                place(block.T, right, total_ref, rows)

    over_depths(chunks, same)
    send_half(total_ref, x_slots, state_x, payload_x)
    over_depths(chunks, functools.partial(cross_part, same_ref, cross_ref, own_y, total_ref, 0))
    send_half(total_ref, y_slots, state_y, payload_y)


def right_kernel(
    sizes_ref, same_ref, cross_ref, upper_ref, own_x, own_y,
    state_x, payload_x, state_y, payload_y, total_ref,
):
    live_rows = sizes_ref[0, TILES]
    for b in range(1, sizes_ref.shape[0]):
        live_rows = live_rows + sizes_ref[b, TILES]
    chunks = chunks_of(live_rows)
    x_slots, y_slots = slot_orders()

    def same(depth):
        for x in range(2):
            place(upper_ref[x * 256 : (x + 1) * 256, :], x, total_ref, slice(None))
        for x in range(2, 4):
            rows = slice(x * 256, (x + 1) * 256)
            result = product(same_ref[:depth, rows], same_ref[:depth, x * 256 :]) + own_x[rows, x * 256 :]
            place(result, x, total_ref, slice((x - 2) * 256, PART))
            if x == 2:
                place(result[:, 256:].T, 3, total_ref, slice(0, 256))

    over_depths(chunks, same)
    send_half(total_ref, x_slots, state_x, payload_x)
    over_depths(chunks, functools.partial(cross_part, same_ref, cross_ref, own_y, total_ref, 1))
    send_half(total_ref, y_slots, state_y, payload_y)


def step_kernel(count, parts, *refs):
    next_ref, payload_ref = refs[2 * parts :]
    half = count // 2
    for part in range(parts):
        state_ref, got_ref = refs[2 * part : 2 * part + 2]
        width = state_ref.shape[2]
        columns = slice(part * width, (part + 1) * width)
        scales = read_scales(got_ref, count)
        for k in range(half):
            next_ref[k, :, columns] = state_ref[k] + read_piece(got_ref, scales, k)

        def load(k, state_ref=state_ref, got_ref=got_ref, scales=scales):
            return state_ref[half + k] + read_piece(got_ref, scales, half + k)

        write_pieces(load, half, payload_ref, columns)


def spread_kernel(parts, *refs):
    next_ref, *payloads = refs[2 * parts :]
    for part in range(parts):
        state_ref, got_ref = refs[2 * part : 2 * part + 2]
        width = state_ref.shape[2]
        columns = slice(part * width, (part + 1) * width)
        scales = read_scales(got_ref, 4)
        next_ref[0, :, columns] = state_ref[0] + read_piece(got_ref, scales, 0)
        for k in range(1, 4):
            piece = state_ref[k] + read_piece(got_ref, scales, k)
            write_pieces(lambda _, piece=piece: piece, 1, payloads[k - 1], columns)


def pack_kernel(*refs):
    *streams, out_ref = refs
    sums = []
    for state_ref, *got in (streams[:4], streams[4:]):
        total = state_ref[0]
        for got_ref in got:
            total = total + read_piece(got_ref, read_scales(got_ref, 1), 0)
        sums.append(total)
    lane = lax.broadcasted_iota(jnp.int32, (16, 128), 1)
    for z in range(8):
        rows = jnp.concatenate([s[z * 8 : (z + 1) * 8, :] for s in sums], axis=0)
        exponents = jnp.zeros((16, 128), jnp.float32)
        for g in range(8):
            values = rows[:, g * 128 : (g + 1) * 128]
            exponent = exponent_of(jnp.max(jnp.abs(values), axis=1, keepdims=True))
            out_ref[z, :, g * 128 : (g + 1) * 128] = to_codes(values, exponent)
            exponents = jnp.where(lane == g, exponent, exponents)
        out_ref[z, :, HALF:] = exponents.astype(jnp.int32).astype(jnp.int16)


def unpack_kernel(got_ref, out_ref):
    total = [jnp.zeros((16, 128), jnp.float32) for _ in range(8)]
    for z in range(8):
        scales = jnp.exp2(got_ref[z, :, HALF:].astype(jnp.int32).astype(jnp.float32)) * (1.0 / FULL)
        for g in range(8):
            codes = got_ref[z, :, g * 128 : (g + 1) * 128].astype(jnp.int32).astype(jnp.float32)
            total[g] = total[g] + codes * scales[:, g : g + 1]
    core = lax.axis_index("core")
    for g in range(8):
        for rows, parity in ((total[g][:8], core), (total[g][8:], 1 - core)):
            out_ref[:, pl.ds(pl.multiple_of((2 * g + parity) * 128, 128), 128)] = rows


VMEM = pl.BlockSpec(memory_space=pltpu.VMEM)
ANY = pl.BlockSpec(memory_space=pl.ANY)
SMEM = pl.BlockSpec(memory_space=pltpu.SMEM)


def call(kernel, inputs, outputs, limit, scratch=(), flops=0, spaces=()):
    moved = sum(int(np.prod(a.shape)) * a.dtype.itemsize for a in (*inputs, *outputs))
    return pl.pallas_call(
        kernel,
        in_specs=[*spaces, *[VMEM] * (len(inputs) - len(spaces))],
        out_specs=[VMEM] * len(outputs),
        out_shape=list(outputs),
        scratch_shapes=list(scratch),
        compiler_params=pltpu.CompilerParams(vmem_limit_bytes=limit << 20),
        cost_estimate=pl.CostEstimate(flops=flops, bytes_accessed=moved, transcendentals=0),
    )(*inputs)


def state_shape(count, width):
    return jax.ShapeDtypeStruct((count, PIECE, width), jnp.float32)


def payload_shape(count, width):
    return jax.ShapeDtypeStruct((count * PIECE + SCALE_ROWS, width), jnp.int16)


def on_device(fitted, screen, block_sizes):
    rows = fitted.shape[0]
    table = jnp.concatenate([screen, block_sizes[:, None]], axis=1)
    other, other_table = swap(fitted, "core"), swap(table, "core")
    square = jax.ShapeDtypeStruct((HALF, HALF), jnp.float32)
    packed = pltpu.VMEM((rows * 48, HALF), jnp.bfloat16)
    mask = pltpu.VMEM((screen.shape[0], 1, 2 * HALF), jnp.float32)
    staged = (pltpu.VMEM(fitted.shape, jnp.bfloat16), pltpu.SemaphoreType.DMA((rows,)))
    total = pltpu.VMEM((16, PIECE, PART), jnp.float32)
    work = 3 * rows * 48 * HALF * HALF
    own = call(
        own_kernel, (fitted, table, table), (square, square), OWN_LIMIT, (mask, packed, packed, *staged), work, (ANY, VMEM, SMEM)
    )
    part = (state_shape(8, PART), payload_shape(8, PART)) * 2
    half = jax.ShapeDtypeStruct((rows * 48, HALF), jnp.bfloat16)
    upper = jax.ShapeDtypeStruct((PART, PART), jnp.float32)
    *left, same, cross, upper = call(
        left_kernel,
        (other, other_table, other_table, *own),
        (*part, half, half, upper),
        OTHER_LIMIT,
        (mask, total),
        work // 2,
        (VMEM, VMEM, SMEM),
    )
    right = call(
        right_kernel, (other_table, same, cross, upper, *own), part, OTHER_LIMIT, (total,), work // 2, (SMEM,)
    )
    states = [left[0], left[2], right[0], right[2]]
    got = [swap(p, step) for p, step in zip((left[1], left[3], right[1], right[3]), ("x1", "y1", "x1", "y1"))]

    def advance(count, width, pairs, step):
        state, payload = call(
            functools.partial(step_kernel, count, len(pairs)),
            tuple(a for pair in pairs for a in pair),
            (state_shape(count // 2, width), payload_shape(count // 2, width)),
            10,
        )
        return state, swap(payload, step)

    moved = [advance(8, PART, [pair], step) for pair, step in zip(zip(states[:2], got[:2]), ("x2", "y2"))]
    *tied, first, second = lax.optimization_barrier((states[2], states[3], moved[0][1], moved[1][1]))
    moved = [(moved[0][0], first), (moved[1][0], second)]
    moved += [advance(8, PART, [pair], step) for pair, step in zip(zip(tied, got[2:]), ("x2", "y2"))]
    streams = []
    for i, axis in enumerate("yx"):
        state, *payloads = call(
            functools.partial(spread_kernel, 2),
            (*moved[i], *moved[i + 2]),
            (state_shape(1, HALF), *[payload_shape(1, HALF)] * 3),
            10,
        )
        streams += [state, *(swap(p, f"{axis}+{k}") for k, p in enumerate(payloads, 1))]
    message = call(
        pack_kernel,
        streams,
        (jax.ShapeDtypeStruct((8, 16, HALF + 128), jnp.int16),),
        4,
    )[0]
    message = lax.all_to_all(message, ("zh", "zl"), 0, 0, tiled=True)
    return call(unpack_kernel, (message,), (jax.ShapeDtypeStruct((8, 2 * HALF), jnp.float32),), 4)[0]


def solution(mesh):
    physical = Mesh(mesh.devices.reshape(SIZES), AXES)
    return jax.shard_map(
        on_device,
        mesh=physical,
        in_specs=(P(("x", "zh", "core"), ("zl", "y"), None), P(("x", "zh", "core"), None), P(("x", "zh", "core"))),
        out_specs=P(AXES, None),
        check_vma=False,
    )
```

```python
import functools

import jax
import jax.numpy as jnp
import numpy as np
from jax import lax
from jax.experimental import pallas as pl
from jax.experimental.pallas import tpu as pltpu
from jax.sharding import Mesh, PartitionSpec as P

AUX_PER_BLOCK = 4
BASIS_PER_TILE = 128
TILES = 16
SIZES = (4, 2, 2, 4, 4)
AXES = ("x", "zh", "core", "zl", "y")
FULL = 32767.0
HALF = 1024
PIECE = 64
PART = 512
OWN_LIMIT = 42
OTHER_LIMIT = 19
SCALE_ROWS = 16


def partner_a(v, core):
    return v ^ 1 if core == 0 else 3 - v


def partner_b(v, core):
    return 3 - v if core == 0 else v ^ 1


PARTNERS = {
    "core": lambda x, y, core: (x, y, 1 - core),
    "x1": lambda x, y, core: (partner_a(x, core), y, core),
    "x2": lambda x, y, core: (partner_b(x, core), y, core),
    "y1": lambda x, y, core: (x, partner_a(y, core), core),
    "y2": lambda x, y, core: (x, partner_b(y, core), core),
    **{f"x+{k}": (lambda x, y, core, k=k: ((x + k) % 4, y, core)) for k in (1, 2, 3)},
    **{f"y+{k}": (lambda x, y, core, k=k: (x, (y + k) % 4, core)) for k in (1, 2, 3)},
}


def swap(value, step):
    pairs = []
    for here in range(256):
        x, zh, core, zl, y = (int(v) for v in np.unravel_index(here, SIZES))
        to_x, to_y, to_core = PARTNERS[step](x, y, core)
        pairs.append((here, int(np.ravel_multi_index((to_x, zh, to_core, zl, to_y), SIZES))))
    return lax.ppermute(value, AXES, pairs)


def exponent_of(largest):
    return jnp.clip(jnp.floor(jnp.log2(largest)) + 1.0, -100.0, 100.0)


def to_codes(values, exponent):
    return jnp.round(values * (jnp.exp2(-exponent) * FULL)).astype(jnp.int32).astype(jnp.int16)


def write_pieces(load, count, payload_ref, columns=slice(None)):
    scales = None
    for k in range(count):
        values = load(k)
        if scales is None:
            row = lax.broadcasted_iota(jnp.int32, (SCALE_ROWS, values.shape[1]), 0)
            scales = jnp.zeros(row.shape, jnp.float32)
        exponent = exponent_of(jnp.max(jnp.abs(values), axis=0, keepdims=True))
        payload_ref[k * PIECE : (k + 1) * PIECE, columns] = to_codes(values, exponent)
        scales = jnp.where(row == k, exponent, scales)
    payload_ref[count * PIECE :, columns] = scales.astype(jnp.int32).astype(jnp.int16)


def read_scales(payload_ref, count):
    exponents = payload_ref[count * PIECE :, :].astype(jnp.int32).astype(jnp.float32)
    return jnp.exp2(exponents) * (1.0 / FULL)


def read_piece(payload_ref, scales, k):
    codes = payload_ref[k * PIECE : (k + 1) * PIECE, :].astype(jnp.int32).astype(jnp.float32)
    return codes * scales[k : k + 1, :]


def place_in_order():
    core = lax.axis_index("core")

    def order(v):
        first = jnp.where(core == 0, v ^ 1, 3 - v)
        second = lambda u: jnp.where(core == 0, 3 - u, u ^ 1)
        return [v, second(v), first, second(first)]

    return core, order(lax.axis_index("x")), order(lax.axis_index("y"))


def load_rows(given, scratch, staged):
    fitted_ref, table_ref, sizes_ref = given
    mask_ref, same_ref, cross_ref = scratch
    core = lax.axis_index("core")
    blocks = table_ref.shape[0]
    live = lambda b, r: sizes_ref[b, TILES] > r

    def copy_of(q):
        return pltpu.make_async_copy(fitted_ref.at[q], staged[0].at[q], staged[1].at[q])

    def fetch(b, carry):
        for r in range(AUX_PER_BLOCK):

            @pl.when(live(b, r))
            def _(r=r):
                copy_of(b * AUX_PER_BLOCK + r).start()

        return carry

    if staged is not None:
        lax.fori_loop(0, blocks, fetch, 0)
    tile = lax.broadcasted_iota(jnp.int32, (16, 2 * HALF), 0)
    column = lax.broadcasted_iota(jnp.int32, (16, 2 * HALF), 1)
    spread = (column // BASIS_PER_TILE == tile).astype(jnp.bfloat16)
    mask = jnp.dot(
        table_ref[:, :TILES].astype(jnp.float32).astype(jnp.bfloat16), spread, preferred_element_type=jnp.float32
    )
    for b in range(blocks):
        mask_ref[b] = mask[b : b + 1, :]
    rows_ref = fitted_ref if staged is None else staged[0]

    def pack(b, first):
        for r in range(AUX_PER_BLOCK):

            @pl.when(live(b, r))
            def _(r=r):
                q = b * AUX_PER_BLOCK + r
                if staged is not None:
                    copy_of(q).wait()
                rows = pl.ds(pl.multiple_of((first + r) * 48, 16), 48)
                for j in range(8):
                    for out_ref, parity in ((same_ref, core), (cross_ref, 1 - core)):
                        lanes = pl.ds(pl.multiple_of((2 * j + parity) * 128, 128), 128)
                        keep = mask_ref[b, :, lanes].astype(jnp.bfloat16)
                        out_ref[rows, j * 128 : (j + 1) * 128] = rows_ref[q, :, lanes] * keep

        return first + sizes_ref[b, TILES]

    first = lax.fori_loop(0, blocks, pack, jnp.int32(0))
    chunks = chunks_of(first)

    def clear(i, carry):
        rows = pl.ds(pl.multiple_of(i * 16, 16), 16)
        same_ref[rows, :] = jnp.zeros((16, HALF), jnp.bfloat16)
        cross_ref[rows, :] = jnp.zeros((16, HALF), jnp.bfloat16)
        return carry

    lax.fori_loop(first * 3, chunks * 16, clear, 0)
    return chunks


def chunks_of(live_rows):
    return jnp.maximum((live_rows * 48 + 255) // 256, 5)


def over_depths(chunks, body):
    for depth in (5, 6):

        @pl.when(chunks == depth)
        def _(depth=depth):
            body(depth * 256)


def product(left, right):
    return lax.dot_general(left, right, (((0,), (0,)), ((), ())), preferred_element_type=jnp.float32)


def place(values, x, out_ref, columns):
    for zh in range(2):
        for zl in range(4):
            for y in range(4):
                source = zh * 128 + zl * 32 + y * 8
                target = (zh * 4 + zl) * 8
                out_ref[x * 4 + y, target : target + 8, columns] = values[source : source + 8, :]


def own_kernel(*refs):
    given, (x_ref, y_ref), scratch, staged = refs[:3], refs[3:5], refs[5:8], refs[8:10]
    same_ref, cross_ref = scratch[1:3]

    def body(depth):
        for x in range(4):
            rows = slice(x * 256, (x + 1) * 256)
            x_ref[rows, x * 256 :] = product(same_ref[:depth, rows], same_ref[:depth, x * 256 :])

        def cross(x, carry):
            rows = pl.ds(pl.multiple_of(x * 256, 256), 256)
            y_ref[rows, :] = product(same_ref[:depth, rows], cross_ref[:depth, :])
            return carry

        lax.fori_loop(0, 4, cross, 0)

    over_depths(load_rows(given, scratch, staged), body)


def send_half(total_ref, slots, state_ref, payload_ref):
    for k in range(8):
        state_ref[k] = total_ref[slots[k]]
    write_pieces(lambda k: total_ref[slots[8 + k]], 8, payload_ref)


def slot_orders():
    _, xs, ys = place_in_order()
    turned = lambda v: [(v + k) % 4 for k in range(4)]
    return [x * 4 + y for x in xs for y in turned(ys[0])], [x * 4 + y for y in ys for x in turned(xs[0])]


def cross_part(same_ref, cross_ref, own_ref, total_ref, part, depth):
    columns = slice(part * PART, (part + 1) * PART)

    def body(x, carry):
        rows = pl.ds(pl.multiple_of(x * 256, 256), 256)
        result = product(same_ref[:depth, rows], cross_ref[:depth, columns]) + own_ref[rows, columns]
        place(result, x, total_ref, slice(None))
        return carry

    lax.fori_loop(0, 4, body, 0, unroll=2 if part else 4)


def left_kernel(
    fitted_ref, table_ref, sizes_ref, own_x, own_y,
    state_x, payload_x, state_y, payload_y, same_ref, cross_ref, upper_ref, mask_ref, total_ref,
):
    chunks = load_rows((fitted_ref, table_ref, sizes_ref), (mask_ref, same_ref, cross_ref), None)
    x_slots, y_slots = slot_orders()

    def same(depth):
        for x in range(2):
            rows = slice(x * 256, (x + 1) * 256)
            result = product(same_ref[:depth, rows], same_ref[:depth, x * 256 :]) + own_x[rows, x * 256 :]
            upper_ref[rows, :] = result[:, -PART:]
            place(result[:, : PART - x * 256], x, total_ref, slice(x * 256, PART))
            for right in range(x + 1, 4):
                block = result[:, (right - x) * 256 : (right - x + 1) * 256]
                place(block.T, right, total_ref, rows)

    over_depths(chunks, same)
    send_half(total_ref, x_slots, state_x, payload_x)
    over_depths(chunks, functools.partial(cross_part, same_ref, cross_ref, own_y, total_ref, 0))
    send_half(total_ref, y_slots, state_y, payload_y)


def right_kernel(
    sizes_ref, same_ref, cross_ref, upper_ref, own_x, own_y,
    state_x, payload_x, state_y, payload_y, total_ref,
):
    live_rows = sizes_ref[0, TILES]
    for b in range(1, sizes_ref.shape[0]):
        live_rows = live_rows + sizes_ref[b, TILES]
    chunks = chunks_of(live_rows)
    x_slots, y_slots = slot_orders()

    def same(depth):
        for x in range(2):
            place(upper_ref[x * 256 : (x + 1) * 256, :], x, total_ref, slice(None))
        for x in range(2, 4):
            rows = slice(x * 256, (x + 1) * 256)
            result = product(same_ref[:depth, rows], same_ref[:depth, x * 256 :]) + own_x[rows, x * 256 :]
            place(result, x, total_ref, slice((x - 2) * 256, PART))
            if x == 2:
                place(result[:, 256:].T, 3, total_ref, slice(0, 256))

    over_depths(chunks, same)
    send_half(total_ref, x_slots, state_x, payload_x)
    over_depths(chunks, functools.partial(cross_part, same_ref, cross_ref, own_y, total_ref, 1))
    send_half(total_ref, y_slots, state_y, payload_y)


def step_kernel(count, parts, *refs):
    next_ref, payload_ref = refs[2 * parts :]
    half = count // 2
    for part in range(parts):
        state_ref, got_ref = refs[2 * part : 2 * part + 2]
        width = state_ref.shape[2]
        columns = slice(part * width, (part + 1) * width)
        scales = read_scales(got_ref, count)
        for k in range(half):
            next_ref[k, :, columns] = state_ref[k] + read_piece(got_ref, scales, k)

        def load(k, state_ref=state_ref, got_ref=got_ref, scales=scales):
            return state_ref[half + k] + read_piece(got_ref, scales, half + k)

        write_pieces(load, half, payload_ref, columns)


def spread_kernel(parts, *refs):
    next_ref, *payloads = refs[2 * parts :]
    for part in range(parts):
        state_ref, got_ref = refs[2 * part : 2 * part + 2]
        width = state_ref.shape[2]
        columns = slice(part * width, (part + 1) * width)
        scales = read_scales(got_ref, 4)
        next_ref[0, :, columns] = state_ref[0] + read_piece(got_ref, scales, 0)
        for k in range(1, 4):
            piece = state_ref[k] + read_piece(got_ref, scales, k)
            write_pieces(lambda _, piece=piece: piece, 1, payloads[k - 1], columns)


def pack_kernel(*refs):
    *streams, out_ref = refs
    sums = []
    for state_ref, *got in (streams[:4], streams[4:]):
        total = state_ref[0]
        for got_ref in got:
            total = total + read_piece(got_ref, read_scales(got_ref, 1), 0)
        sums.append(total)
    lane = lax.broadcasted_iota(jnp.int32, (16, 128), 1)
    for z in range(8):
        rows = jnp.concatenate([s[z * 8 : (z + 1) * 8, :] for s in sums], axis=0)
        exponents = jnp.zeros((16, 128), jnp.float32)
        for g in range(8):
            values = rows[:, g * 128 : (g + 1) * 128]
            exponent = exponent_of(jnp.max(jnp.abs(values), axis=1, keepdims=True))
            out_ref[z, :, g * 128 : (g + 1) * 128] = to_codes(values, exponent)
            exponents = jnp.where(lane == g, exponent, exponents)
        out_ref[z, :, HALF:] = exponents.astype(jnp.int32).astype(jnp.int16)


def unpack_kernel(got_ref, out_ref):
    total = [jnp.zeros((16, 128), jnp.float32) for _ in range(8)]
    for z in range(8):
        scales = jnp.exp2(got_ref[z, :, HALF:].astype(jnp.int32).astype(jnp.float32)) * (1.0 / FULL)
        for g in range(8):
            codes = got_ref[z, :, g * 128 : (g + 1) * 128].astype(jnp.int32).astype(jnp.float32)
            total[g] = total[g] + codes * scales[:, g : g + 1]
    core = lax.axis_index("core")
    for g in range(8):
        for rows, parity in ((total[g][:8], core), (total[g][8:], 1 - core)):
            out_ref[:, pl.ds(pl.multiple_of((2 * g + parity) * 128, 128), 128)] = rows


VMEM = pl.BlockSpec(memory_space=pltpu.VMEM)
ANY = pl.BlockSpec(memory_space=pl.ANY)
SMEM = pl.BlockSpec(memory_space=pltpu.SMEM)


def call(kernel, inputs, outputs, limit, scratch=(), flops=0, spaces=()):
    moved = sum(int(np.prod(a.shape)) * a.dtype.itemsize for a in (*inputs, *outputs))
    return pl.pallas_call(
        kernel,
        in_specs=[*spaces, *[VMEM] * (len(inputs) - len(spaces))],
        out_specs=[VMEM] * len(outputs),
        out_shape=list(outputs),
        scratch_shapes=list(scratch),
        compiler_params=pltpu.CompilerParams(vmem_limit_bytes=limit << 20),
        cost_estimate=pl.CostEstimate(flops=flops, bytes_accessed=moved, transcendentals=0),
    )(*inputs)


def state_shape(count, width):
    return jax.ShapeDtypeStruct((count, PIECE, width), jnp.float32)


def payload_shape(count, width):
    return jax.ShapeDtypeStruct((count * PIECE + SCALE_ROWS, width), jnp.int16)


def on_device(fitted, screen, block_sizes):
    rows = fitted.shape[0]
    table = jnp.concatenate([screen, block_sizes[:, None]], axis=1)
    other, other_table = swap(fitted, "core"), swap(table, "core")
    square = jax.ShapeDtypeStruct((HALF, HALF), jnp.float32)
    packed = pltpu.VMEM((rows * 48, HALF), jnp.bfloat16)
    mask = pltpu.VMEM((screen.shape[0], 1, 2 * HALF), jnp.float32)
    staged = (pltpu.VMEM(fitted.shape, jnp.bfloat16), pltpu.SemaphoreType.DMA((rows,)))
    total = pltpu.VMEM((16, PIECE, PART), jnp.float32)
    work = 3 * rows * 48 * HALF * HALF
    own = call(
        own_kernel, (fitted, table, table), (square, square), OWN_LIMIT, (mask, packed, packed, *staged), work, (ANY, VMEM, SMEM)
    )
    part = (state_shape(8, PART), payload_shape(8, PART)) * 2
    half = jax.ShapeDtypeStruct((rows * 48, HALF), jnp.bfloat16)
    upper = jax.ShapeDtypeStruct((PART, PART), jnp.float32)
    *left, same, cross, upper = call(
        left_kernel,
        (other, other_table, other_table, *own),
        (*part, half, half, upper),
        OTHER_LIMIT,
        (mask, total),
        work // 2,
        (VMEM, VMEM, SMEM),
    )
    right = call(
        right_kernel, (other_table, same, cross, upper, *own), part, OTHER_LIMIT, (total,), work // 2, (SMEM,)
    )
    states = [left[0], left[2], right[0], right[2]]
    got = [swap(p, step) for p, step in zip((left[1], left[3], right[1], right[3]), ("x1", "y1", "x1", "y1"))]

    def advance(count, width, pairs, step):
        state, payload = call(
            functools.partial(step_kernel, count, len(pairs)),
            tuple(a for pair in pairs for a in pair),
            (state_shape(count // 2, width), payload_shape(count // 2, width)),
            10,
        )
        return state, swap(payload, step)

    moved = [advance(8, PART, [pair], step) for pair, step in zip(zip(states[:2], got[:2]), ("x2", "y2"))]
    *tied, first, second = lax.optimization_barrier((states[2], states[3], moved[0][1], moved[1][1]))
    moved = [(moved[0][0], first), (moved[1][0], second)]
    moved += [advance(8, PART, [pair], step) for pair, step in zip(zip(tied, got[2:]), ("x2", "y2"))]
    streams = []
    for i, axis in enumerate("yx"):
        state, *payloads = call(
            functools.partial(spread_kernel, 2),
            (*moved[i], *moved[i + 2]),
            (state_shape(1, HALF), *[payload_shape(1, HALF)] * 3),
            10,
        )
        streams += [state, *(swap(p, f"{axis}+{k}") for k, p in enumerate(payloads, 1))]
    message = call(
        pack_kernel,
        streams,
        (jax.ShapeDtypeStruct((8, 16, HALF + 128), jnp.int16),),
        4,
    )[0]
    message = lax.all_to_all(message, ("zh", "zl"), 0, 0, tiled=True)
    return call(unpack_kernel, (message,), (jax.ShapeDtypeStruct((8, 2 * HALF), jnp.float32),), 4)[0]


def solution(mesh):
    physical = Mesh(mesh.devices.reshape(SIZES), AXES)
    return jax.shard_map(
        on_device,
        mesh=physical,
        in_specs=(P(("x", "zh", "core"), ("zl", "y"), None), P(("x", "zh", "core"), None), P(("x", "zh", "core"))),
        out_specs=P(AXES, None),
        check_vma=False,
    )
```

```python
import functools

import jax
import jax.numpy as jnp
import numpy as np
from jax import lax
from jax.experimental import pallas as pl
from jax.experimental.pallas import tpu as pltpu
from jax.sharding import Mesh, PartitionSpec as P

AUX_PER_BLOCK = 4
BASIS_PER_TILE = 128
TILES = 16
SIZES = (4, 2, 2, 4, 4)
AXES = ("x", "zh", "core", "zl", "y")
FULL = 32767.0
HALF = 1024
PIECE = 64
PART = 512
OWN_LIMIT = 42
OTHER_LIMIT = 19
SCALE_ROWS = 16


def partner_a(v, core):
    return v ^ 1 if core == 0 else 3 - v


def partner_b(v, core):
    return 3 - v if core == 0 else v ^ 1


PARTNERS = {
    "core": lambda x, y, core: (x, y, 1 - core),
    "x1": lambda x, y, core: (partner_a(x, core), y, core),
    "x2": lambda x, y, core: (partner_b(x, core), y, core),
    "y1": lambda x, y, core: (x, partner_a(y, core), core),
    "y2": lambda x, y, core: (x, partner_b(y, core), core),
    **{f"x+{k}": (lambda x, y, core, k=k: ((x + k) % 4, y, core)) for k in (1, 2, 3)},
    **{f"y+{k}": (lambda x, y, core, k=k: (x, (y + k) % 4, core)) for k in (1, 2, 3)},
}


def swap(value, step):
    pairs = []
    for here in range(256):
        x, zh, core, zl, y = (int(v) for v in np.unravel_index(here, SIZES))
        to_x, to_y, to_core = PARTNERS[step](x, y, core)
        pairs.append((here, int(np.ravel_multi_index((to_x, zh, to_core, zl, to_y), SIZES))))
    return lax.ppermute(value, AXES, pairs)


def exponent_of(largest):
    return jnp.clip(jnp.floor(jnp.log2(largest)) + 1.0, -100.0, 100.0)


def to_codes(values, exponent):
    return jnp.round(values * (jnp.exp2(-exponent) * FULL)).astype(jnp.int32).astype(jnp.int16)


def write_pieces(load, count, payload_ref, columns=slice(None)):
    scales = None
    for k in range(count):
        values = load(k)
        if scales is None:
            row = lax.broadcasted_iota(jnp.int32, (SCALE_ROWS, values.shape[1]), 0)
            scales = jnp.zeros(row.shape, jnp.float32)
        exponent = exponent_of(jnp.max(jnp.abs(values), axis=0, keepdims=True))
        payload_ref[k * PIECE : (k + 1) * PIECE, columns] = to_codes(values, exponent)
        scales = jnp.where(row == k, exponent, scales)
    payload_ref[count * PIECE :, columns] = scales.astype(jnp.int32).astype(jnp.int16)


def read_scales(payload_ref, count):
    exponents = payload_ref[count * PIECE :, :].astype(jnp.int32).astype(jnp.float32)
    return jnp.exp2(exponents) * (1.0 / FULL)


def read_piece(payload_ref, scales, k):
    codes = payload_ref[k * PIECE : (k + 1) * PIECE, :].astype(jnp.int32).astype(jnp.float32)
    return codes * scales[k : k + 1, :]


def place_in_order():
    core = lax.axis_index("core")

    def order(v):
        first = jnp.where(core == 0, v ^ 1, 3 - v)
        second = lambda u: jnp.where(core == 0, 3 - u, u ^ 1)
        return [v, second(v), first, second(first)]

    return core, order(lax.axis_index("x")), order(lax.axis_index("y"))


def load_rows(given, scratch, staged):
    fitted_ref, table_ref, sizes_ref = given
    mask_ref, same_ref, cross_ref = scratch
    core = lax.axis_index("core")
    blocks = table_ref.shape[0]
    live = lambda b, r: sizes_ref[b, TILES] > r

    def copy_of(q):
        return pltpu.make_async_copy(fitted_ref.at[q], staged[0].at[q], staged[1].at[q])

    def fetch(b, carry):
        for r in range(AUX_PER_BLOCK):

            @pl.when(live(b, r))
            def _(r=r):
                copy_of(b * AUX_PER_BLOCK + r).start()

        return carry

    if staged is not None:
        lax.fori_loop(0, blocks, fetch, 0)
    tile = lax.broadcasted_iota(jnp.int32, (16, 2 * HALF), 0)
    column = lax.broadcasted_iota(jnp.int32, (16, 2 * HALF), 1)
    spread = (column // BASIS_PER_TILE == tile).astype(jnp.bfloat16)
    mask = jnp.dot(
        table_ref[:, :TILES].astype(jnp.float32).astype(jnp.bfloat16), spread, preferred_element_type=jnp.float32
    )
    for b in range(blocks):
        mask_ref[b] = mask[b : b + 1, :]
    rows_ref = fitted_ref if staged is None else staged[0]

    def pack(b, first):
        for r in range(AUX_PER_BLOCK):

            @pl.when(live(b, r))
            def _(r=r):
                q = b * AUX_PER_BLOCK + r
                if staged is not None:
                    copy_of(q).wait()
                rows = pl.ds(pl.multiple_of((first + r) * 48, 16), 48)
                for j in range(8):
                    for out_ref, parity in ((same_ref, core), (cross_ref, 1 - core)):
                        lanes = pl.ds(pl.multiple_of((2 * j + parity) * 128, 128), 128)
                        keep = mask_ref[b, :, lanes].astype(jnp.bfloat16)
                        out_ref[rows, j * 128 : (j + 1) * 128] = rows_ref[q, :, lanes] * keep

        return first + sizes_ref[b, TILES]

    first = lax.fori_loop(0, blocks, pack, jnp.int32(0), unroll=2)
    chunks = chunks_of(first)

    def clear(i, carry):
        rows = pl.ds(pl.multiple_of(i * 16, 16), 16)
        same_ref[rows, :] = jnp.zeros((16, HALF), jnp.bfloat16)
        cross_ref[rows, :] = jnp.zeros((16, HALF), jnp.bfloat16)
        return carry

    lax.fori_loop(first * 3, chunks * 16, clear, 0)
    return chunks


def chunks_of(live_rows):
    return jnp.maximum((live_rows * 48 + 255) // 256, 5)


def over_depths(chunks, body):
    for depth in (5, 6):

        @pl.when(chunks == depth)
        def _(depth=depth):
            body(depth * 256)


def product(left, right):
    return lax.dot_general(left, right, (((0,), (0,)), ((), ())), preferred_element_type=jnp.float32)


def place(values, x, out_ref, columns):
    for zh in range(2):
        for zl in range(4):
            for y in range(4):
                source = zh * 128 + zl * 32 + y * 8
                target = (zh * 4 + zl) * 8
                out_ref[x * 4 + y, target : target + 8, columns] = values[source : source + 8, :]


def own_kernel(*refs):
    given, (x_ref, y_ref), scratch, staged = refs[:3], refs[3:5], refs[5:8], refs[8:10]
    same_ref, cross_ref = scratch[1:3]

    def body(depth):
        for x in range(4):
            rows = slice(x * 256, (x + 1) * 256)
            x_ref[rows, x * 256 :] = product(same_ref[:depth, rows], same_ref[:depth, x * 256 :])

        def cross(x, carry):
            rows = pl.ds(pl.multiple_of(x * 256, 256), 256)
            y_ref[rows, :] = product(same_ref[:depth, rows], cross_ref[:depth, :])
            return carry

        lax.fori_loop(0, 4, cross, 0, unroll=2)

    over_depths(load_rows(given, scratch, staged), body)


def send_half(total_ref, slots, state_ref, payload_ref):
    for k in range(8):
        state_ref[k] = total_ref[slots[k]]
    write_pieces(lambda k: total_ref[slots[8 + k]], 8, payload_ref)


def slot_orders():
    _, xs, ys = place_in_order()
    turned = lambda v: [(v + k) % 4 for k in range(4)]
    return [x * 4 + y for x in xs for y in turned(ys[0])], [x * 4 + y for y in ys for x in turned(xs[0])]


def cross_part(same_ref, cross_ref, own_ref, total_ref, part, depth):
    columns = slice(part * PART, (part + 1) * PART)

    def body(x, carry):
        rows = pl.ds(pl.multiple_of(x * 256, 256), 256)
        result = product(same_ref[:depth, rows], cross_ref[:depth, columns]) + own_ref[rows, columns]
        place(result, x, total_ref, slice(None))
        return carry

    lax.fori_loop(0, 4, body, 0, unroll=2 if part else 4)


def left_kernel(
    fitted_ref, table_ref, sizes_ref, own_x, own_y,
    state_x, payload_x, state_y, payload_y, same_ref, cross_ref, upper_ref, mask_ref, total_ref,
):
    chunks = load_rows((fitted_ref, table_ref, sizes_ref), (mask_ref, same_ref, cross_ref), None)
    x_slots, y_slots = slot_orders()

    def same(depth):
        for x in range(2):
            rows = slice(x * 256, (x + 1) * 256)
            result = product(same_ref[:depth, rows], same_ref[:depth, x * 256 :]) + own_x[rows, x * 256 :]
            upper_ref[rows, :] = result[:, -PART:]
            place(result[:, : PART - x * 256], x, total_ref, slice(x * 256, PART))
            for right in range(x + 1, 4):
                block = result[:, (right - x) * 256 : (right - x + 1) * 256]
                place(block.T, right, total_ref, rows)

    over_depths(chunks, same)
    send_half(total_ref, x_slots, state_x, payload_x)
    over_depths(chunks, functools.partial(cross_part, same_ref, cross_ref, own_y, total_ref, 0))
    send_half(total_ref, y_slots, state_y, payload_y)


def right_kernel(
    sizes_ref, same_ref, cross_ref, upper_ref, own_x, own_y,
    state_x, payload_x, state_y, payload_y, total_ref,
):
    live_rows = sizes_ref[0, TILES]
    for b in range(1, sizes_ref.shape[0]):
        live_rows = live_rows + sizes_ref[b, TILES]
    chunks = chunks_of(live_rows)
    x_slots, y_slots = slot_orders()

    def same(depth):
        for x in range(2):
            place(upper_ref[x * 256 : (x + 1) * 256, :], x, total_ref, slice(None))
        for x in range(2, 4):
            rows = slice(x * 256, (x + 1) * 256)
            result = product(same_ref[:depth, rows], same_ref[:depth, x * 256 :]) + own_x[rows, x * 256 :]
            place(result, x, total_ref, slice((x - 2) * 256, PART))
            if x == 2:
                place(result[:, 256:].T, 3, total_ref, slice(0, 256))

    over_depths(chunks, same)
    send_half(total_ref, x_slots, state_x, payload_x)
    over_depths(chunks, functools.partial(cross_part, same_ref, cross_ref, own_y, total_ref, 1))
    send_half(total_ref, y_slots, state_y, payload_y)


def step_kernel(count, parts, *refs):
    next_ref, payload_ref = refs[2 * parts :]
    half = count // 2
    for part in range(parts):
        state_ref, got_ref = refs[2 * part : 2 * part + 2]
        width = state_ref.shape[2]
        columns = slice(part * width, (part + 1) * width)
        scales = read_scales(got_ref, count)
        for k in range(half):
            next_ref[k, :, columns] = state_ref[k] + read_piece(got_ref, scales, k)

        def load(k, state_ref=state_ref, got_ref=got_ref, scales=scales):
            return state_ref[half + k] + read_piece(got_ref, scales, half + k)

        write_pieces(load, half, payload_ref, columns)


def spread_kernel(parts, *refs):
    next_ref, *payloads = refs[2 * parts :]
    for part in range(parts):
        state_ref, got_ref = refs[2 * part : 2 * part + 2]
        width = state_ref.shape[2]
        columns = slice(part * width, (part + 1) * width)
        scales = read_scales(got_ref, 4)
        next_ref[0, :, columns] = state_ref[0] + read_piece(got_ref, scales, 0)
        for k in range(1, 4):
            piece = state_ref[k] + read_piece(got_ref, scales, k)
            write_pieces(lambda _, piece=piece: piece, 1, payloads[k - 1], columns)


def pack_kernel(*refs):
    *streams, out_ref = refs
    sums = []
    for state_ref, *got in (streams[:4], streams[4:]):
        total = state_ref[0]
        for got_ref in got:
            total = total + read_piece(got_ref, read_scales(got_ref, 1), 0)
        sums.append(total)
    lane = lax.broadcasted_iota(jnp.int32, (16, 128), 1)
    for z in range(8):
        rows = jnp.concatenate([s[z * 8 : (z + 1) * 8, :] for s in sums], axis=0)
        exponents = jnp.zeros((16, 128), jnp.float32)
        for g in range(8):
            values = rows[:, g * 128 : (g + 1) * 128]
            exponent = exponent_of(jnp.max(jnp.abs(values), axis=1, keepdims=True))
            out_ref[z, :, g * 128 : (g + 1) * 128] = to_codes(values, exponent)
            exponents = jnp.where(lane == g, exponent, exponents)
        out_ref[z, :, HALF:] = exponents.astype(jnp.int32).astype(jnp.int16)


def unpack_kernel(got_ref, out_ref):
    total = [jnp.zeros((16, 128), jnp.float32) for _ in range(8)]
    for z in range(8):
        scales = jnp.exp2(got_ref[z, :, HALF:].astype(jnp.int32).astype(jnp.float32)) * (1.0 / FULL)
        for g in range(8):
            codes = got_ref[z, :, g * 128 : (g + 1) * 128].astype(jnp.int32).astype(jnp.float32)
            total[g] = total[g] + codes * scales[:, g : g + 1]
    core = lax.axis_index("core")
    for g in range(8):
        for rows, parity in ((total[g][:8], core), (total[g][8:], 1 - core)):
            out_ref[:, pl.ds(pl.multiple_of((2 * g + parity) * 128, 128), 128)] = rows


VMEM = pl.BlockSpec(memory_space=pltpu.VMEM)
ANY = pl.BlockSpec(memory_space=pl.ANY)
SMEM = pl.BlockSpec(memory_space=pltpu.SMEM)


def call(kernel, inputs, outputs, limit, scratch=(), flops=0, spaces=()):
    moved = sum(int(np.prod(a.shape)) * a.dtype.itemsize for a in (*inputs, *outputs))
    return pl.pallas_call(
        kernel,
        in_specs=[*spaces, *[VMEM] * (len(inputs) - len(spaces))],
        out_specs=[VMEM] * len(outputs),
        out_shape=list(outputs),
        scratch_shapes=list(scratch),
        compiler_params=pltpu.CompilerParams(vmem_limit_bytes=limit << 20),
        cost_estimate=pl.CostEstimate(flops=flops, bytes_accessed=moved, transcendentals=0),
    )(*inputs)


def state_shape(count, width):
    return jax.ShapeDtypeStruct((count, PIECE, width), jnp.float32)


def payload_shape(count, width):
    return jax.ShapeDtypeStruct((count * PIECE + SCALE_ROWS, width), jnp.int16)


def on_device(fitted, screen, block_sizes):
    rows = fitted.shape[0]
    table = jnp.concatenate([screen, block_sizes[:, None]], axis=1)
    other, other_table = swap(fitted, "core"), swap(table, "core")
    square = jax.ShapeDtypeStruct((HALF, HALF), jnp.float32)
    packed = pltpu.VMEM((rows * 48, HALF), jnp.bfloat16)
    mask = pltpu.VMEM((screen.shape[0], 1, 2 * HALF), jnp.float32)
    staged = (pltpu.VMEM(fitted.shape, jnp.bfloat16), pltpu.SemaphoreType.DMA((rows,)))
    total = pltpu.VMEM((16, PIECE, PART), jnp.float32)
    work = 3 * rows * 48 * HALF * HALF
    own = call(
        own_kernel, (fitted, table, table), (square, square), OWN_LIMIT, (mask, packed, packed, *staged), work, (ANY, VMEM, SMEM)
    )
    part = (state_shape(8, PART), payload_shape(8, PART)) * 2
    half = jax.ShapeDtypeStruct((rows * 48, HALF), jnp.bfloat16)
    upper = jax.ShapeDtypeStruct((PART, PART), jnp.float32)
    *left, same, cross, upper = call(
        left_kernel,
        (other, other_table, other_table, *own),
        (*part, half, half, upper),
        OTHER_LIMIT,
        (mask, total),
        work // 2,
        (VMEM, VMEM, SMEM),
    )
    right = call(
        right_kernel, (other_table, same, cross, upper, *own), part, OTHER_LIMIT, (total,), work // 2, (SMEM,)
    )
    states = [left[0], left[2], right[0], right[2]]
    got = [swap(p, step) for p, step in zip((left[1], left[3], right[1], right[3]), ("x1", "y1", "x1", "y1"))]

    def advance(count, width, pairs, step):
        state, payload = call(
            functools.partial(step_kernel, count, len(pairs)),
            tuple(a for pair in pairs for a in pair),
            (state_shape(count // 2, width), payload_shape(count // 2, width)),
            10,
        )
        return state, swap(payload, step)

    moved = [advance(8, PART, [pair], step) for pair, step in zip(zip(states[:2], got[:2]), ("x2", "y2"))]
    *tied, first, second = lax.optimization_barrier((states[2], states[3], moved[0][1], moved[1][1]))
    moved = [(moved[0][0], first), (moved[1][0], second)]
    moved += [advance(8, PART, [pair], step) for pair, step in zip(zip(tied, got[2:]), ("x2", "y2"))]
    streams = []
    for i, axis in enumerate("yx"):
        state, *payloads = call(
            functools.partial(spread_kernel, 2),
            (*moved[i], *moved[i + 2]),
            (state_shape(1, HALF), *[payload_shape(1, HALF)] * 3),
            10,
        )
        streams += [state, *(swap(p, f"{axis}+{k}") for k, p in enumerate(payloads, 1))]
    message = call(
        pack_kernel,
        streams,
        (jax.ShapeDtypeStruct((8, 16, HALF + 128), jnp.int16),),
        4,
    )[0]
    message = lax.all_to_all(message, ("zh", "zl"), 0, 0, tiled=True)
    return call(unpack_kernel, (message,), (jax.ShapeDtypeStruct((8, 2 * HALF), jnp.float32),), 4)[0]


def solution(mesh):
    physical = Mesh(mesh.devices.reshape(SIZES), AXES)
    return jax.shard_map(
        on_device,
        mesh=physical,
        in_specs=(P(("x", "zh", "core"), ("zl", "y"), None), P(("x", "zh", "core"), None), P(("x", "zh", "core"))),
        out_specs=P(AXES, None),
        check_vma=False,
    )
```

```python
import functools

import jax
import jax.numpy as jnp
import numpy as np
from jax import lax
from jax.experimental import pallas as pl
from jax.experimental.pallas import tpu as pltpu
from jax.sharding import Mesh, PartitionSpec as P

AUX_PER_BLOCK = 4
BASIS_PER_TILE = 128
TILES = 16
SIZES = (4, 2, 2, 4, 4)
AXES = ("x", "zh", "core", "zl", "y")
FULL = 32767.0
HALF = 1024
PIECE = 64
PART = 512
OWN_LIMIT = 42
OTHER_LIMIT = 19
SCALE_ROWS = 16


def partner_a(v, core):
    return v ^ 1 if core == 0 else 3 - v


def partner_b(v, core):
    return 3 - v if core == 0 else v ^ 1


PARTNERS = {
    "core": lambda x, y, core: (x, y, 1 - core),
    "x1": lambda x, y, core: (partner_a(x, core), y, core),
    "x2": lambda x, y, core: (partner_b(x, core), y, core),
    "y1": lambda x, y, core: (x, partner_a(y, core), core),
    "y2": lambda x, y, core: (x, partner_b(y, core), core),
    **{f"x+{k}": (lambda x, y, core, k=k: ((x + k) % 4, y, core)) for k in (1, 2, 3)},
    **{f"y+{k}": (lambda x, y, core, k=k: (x, (y + k) % 4, core)) for k in (1, 2, 3)},
}


def swap(value, step):
    pairs = []
    for here in range(256):
        x, zh, core, zl, y = (int(v) for v in np.unravel_index(here, SIZES))
        to_x, to_y, to_core = PARTNERS[step](x, y, core)
        pairs.append((here, int(np.ravel_multi_index((to_x, zh, to_core, zl, to_y), SIZES))))
    return lax.ppermute(value, AXES, pairs)


def exponent_of(largest):
    return jnp.clip(jnp.floor(jnp.log2(largest)) + 1.0, -100.0, 100.0)


def to_codes(values, exponent):
    return jnp.round(values * (jnp.exp2(-exponent) * FULL)).astype(jnp.int32).astype(jnp.int16)


def write_pieces(load, count, payload_ref, columns=slice(None)):
    scales = None
    for k in range(count):
        values = load(k)
        if scales is None:
            row = lax.broadcasted_iota(jnp.int32, (SCALE_ROWS, values.shape[1]), 0)
            scales = jnp.zeros(row.shape, jnp.float32)
        exponent = exponent_of(jnp.max(jnp.abs(values), axis=0, keepdims=True))
        payload_ref[k * PIECE : (k + 1) * PIECE, columns] = to_codes(values, exponent)
        scales = jnp.where(row == k, exponent, scales)
    payload_ref[count * PIECE :, columns] = scales.astype(jnp.int32).astype(jnp.int16)


def read_scales(payload_ref, count):
    exponents = payload_ref[count * PIECE :, :].astype(jnp.int32).astype(jnp.float32)
    return jnp.exp2(exponents) * (1.0 / FULL)


def read_piece(payload_ref, scales, k):
    codes = payload_ref[k * PIECE : (k + 1) * PIECE, :].astype(jnp.int32).astype(jnp.float32)
    return codes * scales[k : k + 1, :]


def place_in_order():
    core = lax.axis_index("core")

    def order(v):
        first = jnp.where(core == 0, v ^ 1, 3 - v)
        second = lambda u: jnp.where(core == 0, 3 - u, u ^ 1)
        return [v, second(v), first, second(first)]

    return core, order(lax.axis_index("x")), order(lax.axis_index("y"))


def load_rows(given, scratch, staged):
    fitted_ref, table_ref, sizes_ref = given
    mask_ref, same_ref, cross_ref = scratch
    core = lax.axis_index("core")
    blocks = table_ref.shape[0]
    live = lambda b, r: sizes_ref[b, TILES] > r

    def copy_of(q):
        return pltpu.make_async_copy(fitted_ref.at[q], staged[0].at[q], staged[1].at[q])

    def fetch(b, carry):
        for r in range(AUX_PER_BLOCK):

            @pl.when(live(b, r))
            def _(r=r):
                copy_of(b * AUX_PER_BLOCK + r).start()

        return carry

    if staged is not None:
        lax.fori_loop(0, blocks, fetch, 0)
    tile = lax.broadcasted_iota(jnp.int32, (16, 2 * HALF), 0)
    column = lax.broadcasted_iota(jnp.int32, (16, 2 * HALF), 1)
    spread = (column // BASIS_PER_TILE == tile).astype(jnp.bfloat16)
    mask = jnp.dot(
        table_ref[:, :TILES].astype(jnp.float32).astype(jnp.bfloat16), spread, preferred_element_type=jnp.float32
    )
    for b in range(blocks):
        mask_ref[b] = mask[b : b + 1, :]
    rows_ref = fitted_ref if staged is None else staged[0]

    def pack(b, first):
        for r in range(AUX_PER_BLOCK):

            @pl.when(live(b, r))
            def _(r=r):
                q = b * AUX_PER_BLOCK + r
                if staged is not None:
                    copy_of(q).wait()
                rows = pl.ds(pl.multiple_of((first + r) * 48, 16), 48)
                for j in range(8):
                    for out_ref, parity in ((same_ref, core), (cross_ref, 1 - core)):
                        lanes = pl.ds(pl.multiple_of((2 * j + parity) * 128, 128), 128)
                        keep = mask_ref[b, :, lanes].astype(jnp.bfloat16)
                        out_ref[rows, j * 128 : (j + 1) * 128] = rows_ref[q, :, lanes] * keep

        return first + sizes_ref[b, TILES]

    first = lax.fori_loop(0, blocks, pack, jnp.int32(0), unroll=2)
    chunks = chunks_of(first)

    def clear(i, carry):
        rows = pl.ds(pl.multiple_of(i * 16, 16), 16)
        same_ref[rows, :] = jnp.zeros((16, HALF), jnp.bfloat16)
        cross_ref[rows, :] = jnp.zeros((16, HALF), jnp.bfloat16)
        return carry

    lax.fori_loop(first * 3, chunks * 16, clear, 0)
    return chunks


def chunks_of(live_rows):
    return jnp.maximum((live_rows * 48 + 255) // 256, 5)


def over_depths(chunks, body):
    for depth in (5, 6):

        @pl.when(chunks == depth)
        def _(depth=depth):
            body(depth * 256)


def product(left, right):
    return lax.dot_general(left, right, (((0,), (0,)), ((), ())), preferred_element_type=jnp.float32)


def place(values, x, out_ref, columns):
    for zh in range(2):
        for zl in range(4):
            for y in range(4):
                source = zh * 128 + zl * 32 + y * 8
                target = (zh * 4 + zl) * 8
                out_ref[x * 4 + y, target : target + 8, columns] = values[source : source + 8, :]


def own_kernel(*refs):
    given, (x_ref, y_ref), scratch, staged = refs[:3], refs[3:5], refs[5:8], refs[8:10]
    same_ref, cross_ref = scratch[1:3]

    def body(depth):
        for x in range(4):
            rows = slice(x * 256, (x + 1) * 256)
            x_ref[rows, x * 256 :] = product(same_ref[:depth, rows], same_ref[:depth, x * 256 :])

        def cross(x, carry):
            rows = pl.ds(pl.multiple_of(x * 256, 256), 256)
            y_ref[rows, :] = product(same_ref[:depth, rows], cross_ref[:depth, :])
            return carry

        lax.fori_loop(0, 4, cross, 0, unroll=2)

    over_depths(load_rows(given, scratch, staged), body)


def send_half(total_ref, slots, state_ref, payload_ref):
    for k in range(8):
        state_ref[k] = total_ref[slots[k]]
    write_pieces(lambda k: total_ref[slots[8 + k]], 8, payload_ref)


def slot_orders():
    _, xs, ys = place_in_order()
    turned = lambda v: [(v + k) % 4 for k in range(4)]
    return [x * 4 + y for x in xs for y in turned(ys[0])], [x * 4 + y for y in ys for x in turned(xs[0])]


def cross_part(same_ref, cross_ref, own_ref, total_ref, part, depth):
    columns = slice(part * PART, (part + 1) * PART)

    def body(x, carry):
        rows = pl.ds(pl.multiple_of(x * 256, 256), 256)
        result = product(same_ref[:depth, rows], cross_ref[:depth, columns]) + own_ref[rows, columns]
        place(result, x, total_ref, slice(None))
        return carry

    lax.fori_loop(0, 4, body, 0, unroll=2 if part else 4)


def left_kernel(
    fitted_ref, table_ref, sizes_ref, own_x, own_y,
    state_x, payload_x, state_y, payload_y, same_ref, cross_ref, upper_ref, mask_ref, total_ref,
):
    chunks = load_rows((fitted_ref, table_ref, sizes_ref), (mask_ref, same_ref, cross_ref), None)
    x_slots, y_slots = slot_orders()

    def same(depth):
        for x in range(2):
            rows = slice(x * 256, (x + 1) * 256)
            result = product(same_ref[:depth, rows], same_ref[:depth, x * 256 :]) + own_x[rows, x * 256 :]
            upper_ref[rows, :] = result[:, -PART:]
            place(result[:, : PART - x * 256], x, total_ref, slice(x * 256, PART))
            for right in range(x + 1, 4):
                block = result[:, (right - x) * 256 : (right - x + 1) * 256]
                place(block.T, right, total_ref, rows)

    over_depths(chunks, same)
    send_half(total_ref, x_slots, state_x, payload_x)
    over_depths(chunks, functools.partial(cross_part, same_ref, cross_ref, own_y, total_ref, 0))
    send_half(total_ref, y_slots, state_y, payload_y)


def right_kernel(
    sizes_ref, same_ref, cross_ref, upper_ref, own_x, own_y,
    state_x, payload_x, state_y, payload_y, total_ref,
):
    live_rows = sizes_ref[0, TILES]
    for b in range(1, sizes_ref.shape[0]):
        live_rows = live_rows + sizes_ref[b, TILES]
    chunks = chunks_of(live_rows)
    x_slots, y_slots = slot_orders()

    def same(depth):
        for x in range(2):
            place(upper_ref[x * 256 : (x + 1) * 256, :], x, total_ref, slice(None))
        for x in range(2, 4):
            rows = slice(x * 256, (x + 1) * 256)
            result = product(same_ref[:depth, rows], same_ref[:depth, x * 256 :]) + own_x[rows, x * 256 :]
            place(result, x, total_ref, slice((x - 2) * 256, PART))
            if x == 2:
                place(result[:, 256:].T, 3, total_ref, slice(0, 256))

    over_depths(chunks, same)
    send_half(total_ref, x_slots, state_x, payload_x)
    over_depths(chunks, functools.partial(cross_part, same_ref, cross_ref, own_y, total_ref, 1))
    send_half(total_ref, y_slots, state_y, payload_y)


def step_kernel(count, parts, *refs):
    next_ref, payload_ref = refs[2 * parts :]
    half = count // 2
    for part in range(parts):
        state_ref, got_ref = refs[2 * part : 2 * part + 2]
        width = state_ref.shape[2]
        columns = slice(part * width, (part + 1) * width)
        scales = read_scales(got_ref, count)
        for k in range(half):
            next_ref[k, :, columns] = state_ref[k] + read_piece(got_ref, scales, k)

        def load(k, state_ref=state_ref, got_ref=got_ref, scales=scales):
            return state_ref[half + k] + read_piece(got_ref, scales, half + k)

        write_pieces(load, half, payload_ref, columns)


def spread_kernel(parts, *refs):
    next_ref, *payloads = refs[2 * parts :]
    for part in range(parts):
        state_ref, got_ref = refs[2 * part : 2 * part + 2]
        width = state_ref.shape[2]
        columns = slice(part * width, (part + 1) * width)
        scales = read_scales(got_ref, 4)
        next_ref[0, :, columns] = state_ref[0] + read_piece(got_ref, scales, 0)
        for k in range(1, 4):
            piece = state_ref[k] + read_piece(got_ref, scales, k)
            write_pieces(lambda _, piece=piece: piece, 1, payloads[k - 1], columns)


def pack_kernel(*refs):
    *streams, out_ref = refs
    sums = []
    for state_ref, *got in (streams[:4], streams[4:]):
        total = state_ref[0]
        for got_ref in got:
            total = total + read_piece(got_ref, read_scales(got_ref, 1), 0)
        sums.append(total)
    lane = lax.broadcasted_iota(jnp.int32, (16, 128), 1)
    for z in range(8):
        rows = jnp.concatenate([s[z * 8 : (z + 1) * 8, :] for s in sums], axis=0)
        exponents = jnp.zeros((16, 128), jnp.float32)
        for g in range(8):
            values = rows[:, g * 128 : (g + 1) * 128]
            exponent = exponent_of(jnp.max(jnp.abs(values), axis=1, keepdims=True))
            out_ref[z, :, g * 128 : (g + 1) * 128] = to_codes(values, exponent)
            exponents = jnp.where(lane == g, exponent, exponents)
        out_ref[z, :, HALF:] = exponents.astype(jnp.int32).astype(jnp.int16)


def unpack_kernel(got_ref, out_ref):
    total = [jnp.zeros((16, 128), jnp.float32) for _ in range(8)]
    for z in range(8):
        scales = jnp.exp2(got_ref[z, :, HALF:].astype(jnp.int32).astype(jnp.float32)) * (1.0 / FULL)
        for g in range(8):
            codes = got_ref[z, :, g * 128 : (g + 1) * 128].astype(jnp.int32).astype(jnp.float32)
            total[g] = total[g] + codes * scales[:, g : g + 1]
    core = lax.axis_index("core")
    for g in range(8):
        for rows, parity in ((total[g][:8], core), (total[g][8:], 1 - core)):
            out_ref[:, pl.ds(pl.multiple_of((2 * g + parity) * 128, 128), 128)] = rows


VMEM = pl.BlockSpec(memory_space=pltpu.VMEM)
ANY = pl.BlockSpec(memory_space=pl.ANY)
SMEM = pl.BlockSpec(memory_space=pltpu.SMEM)


def call(kernel, inputs, outputs, limit, scratch=(), flops=0, spaces=()):
    moved = sum(int(np.prod(a.shape)) * a.dtype.itemsize for a in (*inputs, *outputs))
    return pl.pallas_call(
        kernel,
        in_specs=[*spaces, *[VMEM] * (len(inputs) - len(spaces))],
        out_specs=[VMEM] * len(outputs),
        out_shape=list(outputs),
        scratch_shapes=list(scratch),
        compiler_params=pltpu.CompilerParams(vmem_limit_bytes=limit << 20),
        cost_estimate=pl.CostEstimate(flops=flops, bytes_accessed=moved, transcendentals=0),
    )(*inputs)


def state_shape(count, width):
    return jax.ShapeDtypeStruct((count, PIECE, width), jnp.float32)


def payload_shape(count, width):
    return jax.ShapeDtypeStruct((count * PIECE + SCALE_ROWS, width), jnp.int16)


def on_device(fitted, screen, block_sizes):
    rows = fitted.shape[0]
    table = jnp.concatenate([screen, block_sizes[:, None]], axis=1)
    other, other_table = swap(fitted, "core"), swap(table, "core")
    square = jax.ShapeDtypeStruct((HALF, HALF), jnp.float32)
    packed = pltpu.VMEM((rows * 48, HALF), jnp.bfloat16)
    mask = pltpu.VMEM((screen.shape[0], 1, 2 * HALF), jnp.float32)
    staged = (pltpu.VMEM(fitted.shape, jnp.bfloat16), pltpu.SemaphoreType.DMA((rows,)))
    total = pltpu.VMEM((16, PIECE, PART), jnp.float32)
    work = 3 * rows * 48 * HALF * HALF
    own = call(
        own_kernel, (fitted, table, table), (square, square), OWN_LIMIT, (mask, packed, packed, *staged), work, (ANY, VMEM, SMEM)
    )
    part = (state_shape(8, PART), payload_shape(8, PART)) * 2
    half = jax.ShapeDtypeStruct((rows * 48, HALF), jnp.bfloat16)
    upper = jax.ShapeDtypeStruct((PART, PART), jnp.float32)
    *left, same, cross, upper = call(
        left_kernel,
        (other, other_table, other_table, *own),
        (*part, half, half, upper),
        OTHER_LIMIT,
        (mask, total),
        work // 2,
        (VMEM, VMEM, SMEM),
    )
    right = call(
        right_kernel, (other_table, same, cross, upper, *own), part, OTHER_LIMIT, (total,), work // 2, (SMEM,)
    )
    states = [left[0], left[2], right[0], right[2]]
    got = [swap(p, step) for p, step in zip((left[1], left[3], right[1], right[3]), ("x1", "y1", "x1", "y1"))]

    def advance(count, width, pairs, step):
        state, payload = call(
            functools.partial(step_kernel, count, len(pairs)),
            tuple(a for pair in pairs for a in pair),
            (state_shape(count // 2, width), payload_shape(count // 2, width)),
            10,
        )
        return state, swap(payload, step)

    moved = [advance(8, PART, [pair], step) for pair, step in zip(zip(states[:2], got[:2]), ("x2", "y2"))]
    *tied, first, second = lax.optimization_barrier((states[2], states[3], moved[0][1], moved[1][1]))
    moved = [(moved[0][0], first), (moved[1][0], second)]
    moved += [advance(8, PART, [pair], step) for pair, step in zip(zip(tied, got[2:]), ("x2", "y2"))]
    streams = []
    for i, axis in enumerate("yx"):
        state, *payloads = call(
            functools.partial(spread_kernel, 2),
            (*moved[i], *moved[i + 2]),
            (state_shape(1, HALF), *[payload_shape(1, HALF)] * 3),
            10,
        )
        streams += [state, *(swap(payloads[k - 1], f"{axis}+{k}") for k in (2, 1, 3))]
    message = call(
        pack_kernel,
        streams,
        (jax.ShapeDtypeStruct((8, 16, HALF + 128), jnp.int16),),
        4,
    )[0]
    message = lax.all_to_all(message, ("zh", "zl"), 0, 0, tiled=True)
    return call(unpack_kernel, (message,), (jax.ShapeDtypeStruct((8, 2 * HALF), jnp.float32),), 4)[0]


def solution(mesh):
    physical = Mesh(mesh.devices.reshape(SIZES), AXES)
    return jax.shard_map(
        on_device,
        mesh=physical,
        in_specs=(P(("x", "zh", "core"), ("zl", "y"), None), P(("x", "zh", "core"), None), P(("x", "zh", "core"))),
        out_specs=P(AXES, None),
        check_vma=False,
    )
```
